512 devices in a mesh: dp: 4 (over z_lo), context: 16 (over x, z_hi), tensor: 8 (over y, core).
Axes of the slice: x: 4, y: 4, z: 16 (z_hi: 4, z_lo: 4; z = z_hi * 4 + z_lo), core: 2. Of those that a mesh axis runs over, the one named last changes fastest.
Arguments:
- queries: bfloat16 [4, 3072, 5120], P('dp', 'context', 'tensor'), may hold values from -80 to 80
- keys: bfloat16 [4, 3072, 1024], P('dp', 'context', 'tensor'), may hold values from -5 to 5
- memory: bfloat16 [4, 3072, 5120], P('dp', 'context'), may hold values from -6 to 6
- value_weight: bfloat16 [5120, 1024], P(None, 'tensor'), may hold values from -0.078125 to 0.078125
- doc_ids: int32 [4, 3072], P('dp'), may hold values from 0 to 7, never falling along the last dimension, each value on 1 to 1536 neighbouring positions
- out_grad: bfloat16 [4, 3072, 5120], P('dp', 'context', 'tensor'), may hold values from -6 to 6
Outputs:
- attended: bfloat16 [4, 3072, 5120], P('dp', 'context', 'tensor')
- grad_queries: bfloat16 [4, 3072, 5120], P('dp', 'context', 'tensor')
- grad_keys: bfloat16 [4, 3072, 1024], P('dp', 'context', 'tensor')
- grad_value_weight: float32 [5120, 1024], P(('dp', 'context'), 'tensor')
The draws below stay inside these ranges and needn't reach their ends.
Inputs may be any that keep to these rules, and one draw needn't show every extreme that they name: `doc_ids`: document numbers never fall along a sequence and every number appears; one document holds exactly 1536 positions.
All inputs are finite; a program needn't handle non-finite values.
Results may differ from the reference program's by a relative error of at most 0.015.
Values may be sent and summed in bfloat16 or wider, within the bound.
A program may use at most 128 MiB of HBM per device.

```python
import math
import jax
import jax.numpy as jnp
import numpy as np
from jax import lax

D = 5120
H = 40
KVH = 8
HD = 128
TOK_DEV = 192
DOCS = 8
GROUP = 5
SEQ = 3072
BATCH = 4
LONGEST = 1536
N_CONTEXT = 16


def key_field(key):
    return jnp.clip(jax.random.normal(key, (BATCH, SEQ, KVH * HD), jnp.float32), -5.0, 5.0)


def draw_keys(key, part):
    return key_field(key).astype(jnp.bfloat16)


def draw_queries(key, part):
    key = jax.random.fold_in(key, 23)
    first_key = jax.random.fold_in(key, 0)
    base = jnp.clip(jax.random.normal(first_key, (BATCH, SEQ, H * HD), jnp.float32), -5.0, 5.0)
    return base.astype(jnp.bfloat16)


def spiked(array, own_key, source, target, shards_of, factor):
    owner, partner = [(jnp.arange(array.shape[axis_at]) // (array.shape[axis_at] // shards_of)).reshape([-1 if axis == axis_at else 1 for axis in range(array.ndim)]) for axis_at in (source, target)]
    chosen = jax.random.permutation(own_key, shards_of)[partner]
    strong = (owner == chosen) | (owner == (partner + shards_of // 2) % shards_of)
    return jnp.where(strong, factor * array, array)


def levels(key, dims, shards, least, largest):
    gain, own = 1.0, jax.random.fold_in(key, 6)
    for axis_at, parts in shards:
        steps = jnp.exp(jax.random.uniform(jax.random.fold_in(own, axis_at), (parts,), jnp.float32, least / len(shards), largest / len(shards)))
        gain = gain * jnp.repeat(steps, dims[axis_at] // parts).reshape([-1 if axis == axis_at else 1 for axis in range(len(dims))])
    return gain


def profile(number_of, total, reach, slope):
    loads = [(1 << 20) // math.isqrt(grade ** slope) + 1 for grade in range(2, number_of + 1)]
    surplus, counts = total - reach - (number_of - 1), [1] * (number_of - 1)
    while surplus > 0:
        candidates = [i for i in range(number_of - 1) if counts[i] < reach]
        pool, budget = sum([loads[i] for i in candidates]), surplus
        for i in candidates:
            more = min(reach - counts[i], max(1, budget * loads[i] // pool), surplus)
            counts[i] = counts[i] + more
            surplus = surplus - more
    return np.array([reach] + counts)


def uneven_parts(rng, count, total, limit, lean):
    if count == 2:
        one = jax.random.randint(rng, (), max(1, total - limit), min(limit, total - 1) + 1)
        return jnp.stack([one, total - one])
    sizes = jnp.asarray(profile(count, total, limit, lean), jnp.int32)
    twos = (count - 1) // 2
    donor, sink = sizes[1:1 + 2 * twos:2], sizes[2:2 + 2 * twos:2]
    margin = jnp.minimum(donor - 1, limit - sink)
    moved = jax.random.randint(jax.random.fold_in(rng, 1), (twos,), 0, 1 << 20) % (margin + 1)
    sizes = sizes.at[1:1 + 2 * twos:2].set(donor - moved).at[2:2 + 2 * twos:2].set(sink + moved)
    return sizes[jax.random.permutation(jax.random.fold_in(rng, 2), count)]


def gaussian(rng, extent, deviation, bound, pieces=(), kind=jnp.bfloat16):
    drawn = deviation * jax.random.normal(rng, extent, jnp.float32)
    if pieces:
        drawn = drawn * levels(rng, extent, pieces, -0.22, 0.18)
    return jnp.clip(drawn, -bound, bound).astype(kind)


def heavy_noise(key, extent, spread, bound, shards, heavy, held_as=jnp.bfloat16):
    values = spread * jax.random.normal(key, extent, jnp.float32)
    if shards:
        values = values * levels(key, extent, shards, -0.22, 0.18)
    return jnp.clip(spiked(values, jax.random.fold_in(key, 3), *heavy), -bound, bound).astype(held_as)


def setup_inputs(seed: int = 0) -> dict:
    key_list = jax.random.split(jax.random.key(seed), 7)
    return {
        "queries": draw_queries(jax.random.fold_in(key_list[6], 71), 0),
        "keys": draw_keys(jax.random.fold_in(key_list[6], 71), 0),
        "memory": heavy_noise(key_list[2], (BATCH, SEQ, D), 1.0, 6.0, ((0, 4), (1, 16)), (1, 2, 16, 2.0)),
        "value_weight": gaussian(key_list[3], (D, KVH * HD), D ** -0.5, 0.078125, ((1, 8),)),
        "doc_ids": jax.vmap(lambda own: jnp.searchsorted(jnp.cumsum(uneven_parts(own, DOCS, SEQ, LONGEST, 1)), jnp.arange(SEQ), side="right"))(jax.random.split(key_list[4], BATCH)).reshape((BATCH, SEQ)).astype(jnp.int32),
        "out_grad": gaussian(key_list[5], (BATCH, SEQ, H * HD), 1.0, 6.0, ((0, 4), (1, 16), (2, 8))),
    }


NEG_FILL = -1e30


def group_pass(q_group, k_group, v_group, g_group, doc_row):
    positions = jnp.arange(SEQ)
    visible = (doc_row[:, None] == doc_row[None, :]) & (positions[None, :] <= positions[:, None])
    q_float = q_group.astype(jnp.float32)
    k_float = k_group.astype(jnp.float32)
    v_float = v_group.astype(jnp.float32)
    g_float = g_group.astype(jnp.float32)
    score_scale = HD ** -0.5
    scores = jnp.einsum("qjd,kd->qjk", q_float, k_float) * score_scale
    scores = jnp.where(visible[:, None, :], scores, NEG_FILL)
    row_top = jnp.max(scores, axis=-1, keepdims=True)
    exp_rows = jnp.exp(scores - row_top)
    softmax_rows = exp_rows / jnp.sum(exp_rows, axis=-1, keepdims=True)
    probs_half = softmax_rows.astype(jnp.bfloat16)
    attended = jnp.einsum("qjk,kd->qjd", probs_half.astype(jnp.float32), v_float).astype(jnp.bfloat16)
    grad_probs = jnp.einsum("qjd,kd->qjk", g_float, v_float)
    row_delta = jnp.sum(g_float * attended.astype(jnp.float32), axis=-1, keepdims=True)
    grad_scores = (softmax_rows * (grad_probs - row_delta) * score_scale).astype(jnp.bfloat16)
    grad_query = jnp.einsum("qjk,kd->qjd", grad_scores.astype(jnp.float32), k_float).astype(jnp.bfloat16)
    shard_scores = grad_scores.astype(jnp.float32).reshape(N_CONTEXT, TOK_DEV, GROUP, SEQ)
    shard_probs = probs_half.astype(jnp.float32).reshape(N_CONTEXT, TOK_DEV, GROUP, SEQ)
    shard_query = q_float.reshape(N_CONTEXT, TOK_DEV, GROUP, HD)
    shard_grad = g_float.reshape(N_CONTEXT, TOK_DEV, GROUP, HD)
    key_parts = jnp.einsum("cqjk,cqjd->ckd", shard_scores, shard_query).astype(jnp.bfloat16)
    value_parts = jnp.einsum("cqjk,cqjd->ckd", shard_probs, shard_grad).astype(jnp.bfloat16)
    key_parts = lax.optimization_barrier(key_parts)
    value_parts = lax.optimization_barrier(value_parts)
    grad_key = jnp.sum(key_parts.astype(jnp.float32), axis=0).astype(jnp.bfloat16)
    grad_value = jnp.sum(value_parts.astype(jnp.float32), axis=0).astype(jnp.bfloat16)
    return attended, grad_query, grad_key, grad_value


def reference(queries, keys, memory, value_weight, doc_ids, out_grad):
    values = jnp.dot(memory.reshape(BATCH * SEQ, D), value_weight, preferred_element_type=jnp.float32)
    values = values.astype(jnp.bfloat16).reshape(BATCH, SEQ, KVH, HD)
    attended_rows = []
    query_rows = []
    key_rows = []
    value_rows = []
    for row_index in range(BATCH):
        q_row = queries[row_index].reshape(SEQ, KVH, GROUP, HD).transpose(1, 0, 2, 3)
        k_row = keys[row_index].reshape(SEQ, KVH, HD).transpose(1, 0, 2)
        v_row = values[row_index].transpose(1, 0, 2)
        g_row = out_grad[row_index].reshape(SEQ, KVH, GROUP, HD).transpose(1, 0, 2, 3)
        doc_row = doc_ids[row_index]
        result = lax.map(lambda packed: group_pass(packed[0], packed[1], packed[2], packed[3], doc_row),
                         (q_row, k_row, v_row, g_row))
        attended_rows.append(result[0].transpose(1, 0, 2, 3).reshape(SEQ, H * HD))
        query_rows.append(result[1].transpose(1, 0, 2, 3).reshape(SEQ, H * HD))
        key_rows.append(result[2].transpose(1, 0, 2).reshape(SEQ, KVH * HD))
        value_rows.append(result[3].transpose(1, 0, 2).reshape(SEQ, KVH * HD))
    attended = jnp.stack(attended_rows)
    grad_queries = jnp.stack(query_rows)
    grad_keys = jnp.stack(key_rows)
    grad_values = jnp.stack(value_rows)
    grad_value_weight = lax.dot_general(memory.reshape(BATCH * SEQ, D), grad_values.reshape(BATCH * SEQ, KVH * HD),
                                        (((0,), (0,)), ((), ())), preferred_element_type=jnp.float32)
    return (attended, grad_queries, grad_keys, grad_value_weight)
```

```python
import math

import jax
import jax.numpy as jnp
from jax import lax
from jax.experimental import pallas as pl
from jax.experimental.pallas import tpu as pltpu
from jax.sharding import PartitionSpec as P

MESH = pl.DeviceIdType.MESH
BF = jnp.bfloat16
F32 = jnp.float32

HD = 128
TOK = 192
HALF = TOK // 2
HEADS = 5
D = 5120
SEQ = 3072
NX = 4
NZ = 4
NDP = 4
SPAN = 8
LANES = 1024
CHUNK = 256
ROWS_X = D // (NDP * NX)
ROWS_OUT = ROWS_X // NZ
SCALE = HD ** (-0.5)
LOG2E = math.log2(math.e)
NEG = -1e30


def dot(a, b):
    return jnp.dot(a, b, preferred_element_type=F32)


def remote(src, dst, send, recv, device):
    return pltpu.make_async_remote_copy(
        src_ref=src, dst_ref=dst, send_sem=send, recv_sem=recv, device_id=device, device_id_type=MESH
    )


def kernel(
    q_hbm, k_hbm, mem_hbm, w_hbm, doc_hbm, g_hbm,
    att_hbm, gq_hbm, gk_hbm, gw_hbm,
    q_in, g_in, mem, w, doc,
    kv, qall, gall, gnorm, qt, gt, memt,
    sbuf, pbuf, top, total, ot, dqt, out_rows, grad_rows,
    part, from_x, acc, zsend, from_z, gk_out, dv,
    wsend, wown, wrecv, dsend, dacc, drecv, hsend, hrecv, gw_out,
    lsem, gs, gr, xs, xr, zs, zr, ws, wr, ds, dr, hs, hr,
):
    c = lax.axis_index("context")
    dp = lax.axis_index("dp")
    x = c // NZ
    zh = c % NZ

    def zat(j):
        return lax.rem(zh + j, NZ)

    def zdev(j):
        return {"context": x * NZ + zat(j)}

    def xdev(j):
        return {"context": lax.rem(c + NZ * j, NX * NZ)}

    def dpdev(j):
        return {"dp": lax.rem(dp + j, NDP)}

    loads = [
        pltpu.make_async_copy(k_hbm.at[0], kv.at[0, 0, zh], lsem.at[0]),
        pltpu.make_async_copy(mem_hbm.at[0], mem, lsem.at[1]),
        pltpu.make_async_copy(w_hbm, w, lsem.at[2]),
        pltpu.make_async_copy(q_hbm.at[0], q_in, lsem.at[3]),
        pltpu.make_async_copy(g_hbm.at[0], g_in, lsem.at[4]),
        pltpu.make_async_copy(doc_hbm, doc, lsem.at[5]),
    ]
    for load in loads:
        load.start()

    barrier = pltpu.get_barrier_semaphore()
    for j in range(1, 4):
        for device in (zdev(j), xdev(j), dpdev(j)):
            pl.semaphore_signal(barrier, inc=1, device_id=device, device_id_type=MESH)

    def ring(a, i):
        row = kv.at[a, 0]
        if i == 0:
            return remote(row.at[zh], row.at[zh], gs.at[a, 0], gr.at[a, 0], zdev(1))
        if i == 1:
            return remote(row.at[zh], row.at[zh], gs.at[a, 1], gr.at[a, 1], zdev(3))
        if i == 2:
            half = row.at[zat(3), pl.ds(0, HALF)]
            return remote(half, half, gs.at[a, 2], gr.at[a, 2], zdev(1))
        half = row.at[zat(1), pl.ds(HALF, HALF)]
        return remote(half, half, gs.at[a, 3], gr.at[a, 3], zdev(3))

    def down(a, r, j):
        z = zat(j)
        return remote(
            kv.at[a, 0, z], kv.at[a, r, z], gs.at[a, 4 * r + j], gr.at[a, 4 * r + j], xdev(r)
        )

    def down_all(a, j, act):
        @pl.when(x < NX - 1)
        def _():
            act(down(a, 1, j))

        @pl.when((x < NX - 2) & (zat(j) >= zh))
        def _():
            act(down(a, 2, j))

    def from_above(a):
        for j in range(NZ):
            @pl.when(x > 0)
            def _():
                down(a, 1, j).wait_recv()

            @pl.when((x > 1) & (zat(j) >= zh))
            def _():
                down(a, 2, j).wait_recv()

    def start(copy):
        copy.start()

    def wait_send(copy):
        copy.wait_send()

    loads[0].wait()
    pl.semaphore_wait(barrier, 9)
    ring(0, 0).start()
    ring(0, 1).start()
    down_all(0, 0, start)

    loads[1].wait()
    loads[2].wait()
    kv[1, 0, zh] = dot(mem[...], w[...]).astype(BF)
    ring(1, 0).start()
    ring(1, 1).start()
    down_all(1, 0, start)

    loads[3].wait()
    loads[4].wait()
    loads[5].wait()
    for h in range(HEADS):
        qall[TOK * h : TOK * (h + 1), :] = q_in[:, HD * h : HD * (h + 1)]
        gall[TOK * h : TOK * (h + 1), :] = g_in[:, HD * h : HD * (h + 1)]
    pad = jnp.zeros((LANES - HEADS * TOK, HD), BF)
    qall[HEADS * TOK :, :] = pad
    gall[HEADS * TOK :, :] = pad
    qt[...] = qall[...].T
    gt[...] = gall[...].T

    doc_row = doc[...].astype(F32)
    pair = doc[:, pl.ds(pl.multiple_of(2 * TOK * (c // 2), 128), 2 * TOK)].astype(F32)
    doc_q = jnp.where(c % 2 == 0, pair[:, :TOK], pair[:, TOK:])
    first = jnp.zeros((1, TOK), F32)
    for d in range(1, 8):
        before = jnp.sum(jnp.where(doc_row < d, 1.0, 0.0), axis=1, keepdims=True)
        first = jnp.where(doc_q == d, before, first)
    own_pos = lax.broadcasted_iota(jnp.int32, (1, TOK), 1).astype(F32) + (c * TOK).astype(F32)
    lane_pad = LANES - HEADS * TOK
    q_first = jnp.concatenate([first] * HEADS + [jnp.zeros((1, lane_pad), F32)], axis=1)
    q_pos = jnp.concatenate([own_pos] * HEADS + [jnp.full((1, lane_pad), float(SEQ), F32)], axis=1)

    part[:, 0] = jnp.zeros((2, NZ, TOK, HD), BF)
    top[...] = jnp.full((8, LANES), NEG, F32)
    total[...] = jnp.zeros((8, LANES), F32)

    blocks = jnp.minimum(c, SPAN) + 1

    def slot(d):
        b = c - d
        return x - b // NZ, b % NZ

    def scores(d, carry):
        r, z = slot(d)
        kb = kv[0, r, z]
        key_pos = lax.broadcasted_iota(jnp.int32, (TOK, CHUNK), 0).astype(F32) + (
            (c - d) * TOK
        ).astype(F32)
        for i in range(LANES // CHUNK):
            at = slice(CHUNK * i, CHUNK * (i + 1))
            s = dot(kb, qt[:, at])
            s = jnp.where((key_pos >= q_first[:, at]) & (key_pos <= q_pos[:, at]), s, NEG)
            sbuf[d, :, at] = s
            top[:, at] = jnp.maximum(top[:, at], jnp.max(s.reshape(TOK // 8, 8, CHUNK), axis=0))
        return carry

    ring(0, 0).wait_recv()
    ring(0, 2).start()
    ring(0, 1).wait_recv()
    ring(0, 3).start()
    down_all(0, 1, start)
    down_all(0, 3, start)
    ring(1, 0).wait_recv()
    ring(1, 2).start()
    ring(1, 1).wait_recv()
    ring(1, 3).start()
    down_all(1, 1, start)
    down_all(1, 3, start)
    ring(0, 2).wait_recv()
    ring(0, 3).wait_recv()
    down_all(0, 2, start)
    lax.fori_loop(0, jnp.minimum(zh + 1, blocks), scores, 0)
    memt[...] = mem[...].T
    ring(1, 2).wait_recv()
    ring(1, 3).wait_recv()
    down_all(1, 2, start)
    from_above(0)
    lax.fori_loop(jnp.minimum(zh + 1, blocks), blocks, scores, 0)

    top_row = jnp.max(top[...], axis=0, keepdims=True) * (SCALE * LOG2E)

    def numerators(d, carry):
        for i in range(LANES // CHUNK):
            at = slice(CHUNK * i, CHUNK * (i + 1))
            e = jnp.exp2(sbuf[d, :, at] * (SCALE * LOG2E) - top_row[:, at])
            sbuf[d, :, at] = e
            pbuf[d, :, at] = e.astype(BF)
            total[:, at] += jnp.sum(e.reshape(TOK // 8, 8, CHUNK), axis=0)
        return carry

    lax.fori_loop(0, blocks, numerators, 0)
    inv = 1.0 / jnp.sum(total[...], axis=0, keepdims=True)
    inv_col = jnp.broadcast_to(inv, (HD, LANES)).T
    gnorm[...] = (gall[...].astype(F32) * inv_col).astype(BF)

    def up(a, r, j):
        z = zat(j)
        return remote(
            part.at[a, r, z], from_x.at[a, r - 1, z], xs.at[a, 4 * (r - 1) + j],
            xr.at[a, 4 * (r - 1) + j], xdev(NX - r),
        )

    def up_all(a, act):
        for j in range(NZ):
            @pl.when(x > 0)
            def _():
                act(up(a, 1, j))

            @pl.when((x > 1) & (zat(j) >= zh))
            def _():
                act(up(a, 2, j))

    def over(a, j):
        return remote(zsend.at[a, zat(j)], from_z.at[a, j], zs.at[a, j], zr.at[a, j], zdev(j))

    def sum_rows(a):
        for j in (2, 1, 3, 0):
            z = zat(j)
            acc[...] = part[a, 0, z].astype(F32)

            @pl.when(x < NX - 1)
            def _():
                up(a, 1, j).wait_recv()
                acc[...] += from_x[a, 0, z].astype(F32)

            @pl.when((x < NX - 2) & (z >= zh))
            def _():
                up(a, 2, j).wait_recv()
                acc[...] += from_x[a, 1, z].astype(F32)

            if j:
                zsend[a, z] = acc[...].astype(BF)
                over(a, j).start()
            else:
                part[a, 0, z] = acc[...].astype(BF)

    def sum_ring(a):
        out = part[a, 0, zh].astype(F32)
        for j in (1, 3, 2):
            over(a, j).wait_recv()
            out = out + from_z[a, j].astype(F32)
        return out.astype(BF)

    def value_parts(d, carry):
        r, z = slot(d)
        part[1, r, z] = dot(pbuf[d], gnorm[...]).astype(BF)
        return carry

    lax.fori_loop(0, blocks, value_parts, 0)
    up_all(1, start)

    from_above(1)
    ot[...] = jnp.zeros((HD, LANES), F32)

    def attend(d, carry):
        r, z = slot(d)
        ot[...] += dot(kv[1, r, z].T, pbuf[d])
        return carry

    lax.fori_loop(0, blocks, attend, 0)
    att = (ot[...] * inv).astype(BF).astype(F32)
    delta = jnp.sum(att * gt[...].astype(F32), axis=0, keepdims=True)
    att_rows = att.T.astype(BF)
    for h in range(HEADS):
        out_rows[:, HD * h : HD * (h + 1)] = att_rows[TOK * h : TOK * (h + 1), :]
    store_att = pltpu.make_async_copy(out_rows, att_hbm.at[0], lsem.at[6])
    store_att.start()

    sum_rows(1)

    dqt[...] = jnp.zeros((HD, LANES), F32)
    inv_scaled = inv * SCALE

    def grads(d, carry):
        r, z = slot(d)
        vb = kv[1, r, z]
        kt = kv[0, r, z].T
        for i in range(LANES // CHUNK):
            at = slice(CHUNK * i, CHUNK * (i + 1))
            dprob = dot(vb, gt[:, at])
            pbuf[d, :, at] = (sbuf[d, :, at] * ((dprob - delta[:, at]) * inv_scaled[:, at])).astype(BF)
        part[0, r, z] = dot(pbuf[d], qall[...]).astype(BF)
        dqt[...] += dot(kt, pbuf[d])
        return carry

    lax.fori_loop(0, blocks, grads, 0)
    up_all(0, start)
    dq_rows = dqt[...].T.astype(BF)
    for h in range(HEADS):
        grad_rows[:, HD * h : HD * (h + 1)] = dq_rows[TOK * h : TOK * (h + 1), :]
    store_gq = pltpu.make_async_copy(grad_rows, gq_hbm.at[0], lsem.at[7])
    store_gq.start()

    sum_rows(0)
    dv[...] = sum_ring(1)

    def wx(k, o):
        return remote(wsend.at[k, o], wrecv.at[k, o], ws.at[k, o], wr.at[k, o], xdev(o))

    def wd(k):
        return remote(dsend.at[k], drecv.at[k], ds.at[k], dr.at[k], dpdev(k + 1))

    def wh(o):
        return remote(hsend.at[o], hrecv.at[o], hs.at[o], hr.at[o], zdev(o))

    for k in range(NDP):
        for o in (2, 1, 3, 0):
            row = NX * ROWS_X * lax.rem(dp + 1 + k, NDP) + ROWS_X * lax.rem(x + o, NX)
            piece = dot(memt[pl.ds(pl.multiple_of(row, 64), ROWS_X), :], dv[...])
            if o:
                wsend[k, o] = piece.astype(BF)
                wx(k, o).start()
            else:
                wown[k] = piece

    gk_out[...] = sum_ring(0)
    store_gk = pltpu.make_async_copy(gk_out, gk_hbm.at[0], lsem.at[8])
    store_gk.start()

    for k in range(NDP):
        piece = wown[k]
        for o in (1, 3, 2):
            wx(k, o).wait_recv()
            piece = piece + wrecv[k, o].astype(F32)
        if k < NDP - 1:
            dsend[k] = piece.astype(BF)
            wd(k).start()
        else:
            dacc[...] = piece
    for k in range(NDP - 1):
        wd(k).wait_recv()
        dacc[...] += drecv[k].astype(F32)
    for o in (2, 1, 3):
        rows = pl.ds(pl.multiple_of(ROWS_OUT * zat(o), 16), ROWS_OUT)
        hsend[o] = dacc[rows, :].astype(BF)
        wh(o).start()
    out = dacc[pl.ds(pl.multiple_of(ROWS_OUT * zh, 16), ROWS_OUT), :]
    for o in (1, 3, 2):
        wh(o).wait_recv()
        out = out + hrecv[o].astype(F32)
    gw_out[...] = out
    store_gw = pltpu.make_async_copy(gw_out, gw_hbm, lsem.at[9])
    store_gw.start()

    for a in range(2):
        for i in range(4):
            ring(a, i).wait_send()
        for j in range(NZ):
            down_all(a, j, wait_send)
        up_all(a, wait_send)
        for j in range(1, NZ):
            over(a, j).wait_send()
    for k in range(NDP):
        for o in range(1, NX):
            wx(k, o).wait_send()
    for k in range(NDP - 1):
        wd(k).wait_send()
    for o in range(1, NZ):
        wh(o).wait_send()
    for store in (store_att, store_gq, store_gk, store_gw):
        store.wait()


def on_device(queries, keys, memory, value_weight, doc_ids, out_grad):
    vmem = pltpu.VMEM
    dma = pltpu.SemaphoreType.DMA
    anywhere = pl.BlockSpec(memory_space=pl.ANY)
    shape = jax.ShapeDtypeStruct
    return pl.pallas_call(
        kernel,
        out_shape=(
            shape((1, TOK, HEADS * HD), BF),
            shape((1, TOK, HEADS * HD), BF),
            shape((1, TOK, HD), BF),
            shape((ROWS_OUT, HD), F32),
        ),
        in_specs=[anywhere] * 6,
        out_specs=(anywhere,) * 4,
        scratch_shapes=[
            vmem((TOK, HEADS * HD), BF),
            vmem((TOK, HEADS * HD), BF),
            vmem((TOK, D), BF),
            vmem((D, HD), BF),
            vmem((1, SEQ), jnp.int32),
            vmem((2, 3, NZ, TOK, HD), BF),
            vmem((LANES, HD), BF),
            vmem((LANES, HD), BF),
            vmem((LANES, HD), BF),
            vmem((HD, LANES), BF),
            vmem((HD, LANES), BF),
            vmem((D, TOK), BF),
            vmem((SPAN + 1, TOK, LANES), F32),
            vmem((SPAN + 1, TOK, LANES), BF),
            vmem((8, LANES), F32),
            vmem((8, LANES), F32),
            vmem((HD, LANES), F32),
            vmem((HD, LANES), F32),
            vmem((TOK, HEADS * HD), BF),
            vmem((TOK, HEADS * HD), BF),
            vmem((2, 3, NZ, TOK, HD), BF),
            vmem((2, 2, NZ, TOK, HD), BF),
            vmem((TOK, HD), F32),
            vmem((2, NZ, TOK, HD), BF),
            vmem((2, NZ, TOK, HD), BF),
            vmem((TOK, HD), BF),
            vmem((TOK, HD), BF),
            vmem((NDP, NX, ROWS_X, HD), BF),
            vmem((NDP, ROWS_X, HD), F32),
            vmem((NDP, NX, ROWS_X, HD), BF),
            vmem((NDP, ROWS_X, HD), BF),
            vmem((ROWS_X, HD), F32),
            vmem((NDP, ROWS_X, HD), BF),
            vmem((NZ, ROWS_OUT, HD), BF),
            vmem((NZ, ROWS_OUT, HD), BF),
            vmem((ROWS_OUT, HD), F32),
            dma((10,)),
            dma((2, 12)), dma((2, 12)),
            dma((2, 8)), dma((2, 8)),
            dma((2, NZ)), dma((2, NZ)),
            dma((NDP, NX)), dma((NDP, NX)),
            dma((NDP,)), dma((NDP,)),
            dma((NZ,)), dma((NZ,)),
        ],
        compiler_params=pltpu.CompilerParams(
            collective_id=0, has_side_effects=True, vmem_limit_bytes=48 << 20
        ),
        name="cross_attention",
    )(queries, keys, memory, value_weight, doc_ids, out_grad)


def solution(mesh):
    in_specs = (
        P("dp", "context", "tensor"),
        P("dp", "context", "tensor"),
        P("dp", "context", None),
        P(None, "tensor"),
        P("dp", None),
        P("dp", "context", "tensor"),
    )
    out_specs = (
        P("dp", "context", "tensor"),
        P("dp", "context", "tensor"),
        P("dp", "context", "tensor"),
        P(("dp", "context"), "tensor"),
    )
    return jax.shard_map(
        on_device, mesh=mesh, in_specs=in_specs, out_specs=out_specs, check_vma=False
    )
```

```python
import math

import jax
import jax.numpy as jnp
from jax import lax
from jax.experimental import pallas as pl
from jax.experimental.pallas import tpu as pltpu
from jax.sharding import PartitionSpec as P

MESH = pl.DeviceIdType.MESH
BF = jnp.bfloat16
F32 = jnp.float32

HD = 128
TOK = 192
HALF = TOK // 2
HEADS = 5
D = 5120
SEQ = 3072
NX = 4
NZ = 4
NDP = 4
SPAN = 8
LANES = 1024
CHUNK = 256
ROWS_X = D // (NDP * NX)
ROWS_OUT = ROWS_X // NZ
SCALE = HD ** (-0.5)
LOG2E = math.log2(math.e)
NEG = -1e30


def dot(a, b):
    return jnp.dot(a, b, preferred_element_type=F32)


def remote(src, dst, send, recv, device):
    return pltpu.make_async_remote_copy(
        src_ref=src, dst_ref=dst, send_sem=send, recv_sem=recv, device_id=device, device_id_type=MESH
    )


def kernel(
    q_hbm, k_hbm, mem_hbm, w_hbm, doc_hbm, g_hbm,
    att_hbm, gq_hbm, gk_hbm, gw_hbm,
    q_in, g_in, mem, w, doc,
    kv, qall, gall, gnorm, qt, gt, memt,
    sbuf, pbuf, top, total, ot, dqt, out_rows, grad_rows,
    part, from_x, acc, zsend, from_z, gk_out, dv,
    wsend, wown, wrecv, dsend, dacc, drecv, hsend, hrecv, gw_out,
    lsem, gs, gr, xs, xr, zs, zr, ws, wr, ds, dr, hs, hr,
):
    c = lax.axis_index("context")
    dp = lax.axis_index("dp")
    x = c // NZ
    zh = c % NZ

    def zat(j):
        return lax.rem(zh + j, NZ)

    def zdev(j):
        return {"context": x * NZ + zat(j)}

    def xdev(j):
        return {"context": lax.rem(c + NZ * j, NX * NZ)}

    def dpdev(j):
        return {"dp": lax.rem(dp + j, NDP)}

    loads = [
        pltpu.make_async_copy(k_hbm.at[0], kv.at[0, 0, zh], lsem.at[0]),
        pltpu.make_async_copy(mem_hbm.at[0], mem, lsem.at[1]),
        pltpu.make_async_copy(w_hbm, w, lsem.at[2]),
        pltpu.make_async_copy(q_hbm.at[0], q_in, lsem.at[3]),
        pltpu.make_async_copy(g_hbm.at[0], g_in, lsem.at[4]),
        pltpu.make_async_copy(doc_hbm, doc, lsem.at[5]),
    ]
    for load in loads:
        load.start()

    barrier = pltpu.get_barrier_semaphore()
    for j in range(1, 4):
        for device in (zdev(j), xdev(j), dpdev(j)):
            pl.semaphore_signal(barrier, inc=1, device_id=device, device_id_type=MESH)

    def ring(a, i):
        row = kv.at[a, 0]
        if i == 0:
            return remote(row.at[zh], row.at[zh], gs.at[a, 0], gr.at[a, 0], zdev(1))
        if i == 1:
            return remote(row.at[zh], row.at[zh], gs.at[a, 1], gr.at[a, 1], zdev(3))
        if i == 2:
            half = row.at[zat(3), pl.ds(0, HALF)]
            return remote(half, half, gs.at[a, 2], gr.at[a, 2], zdev(1))
        half = row.at[zat(1), pl.ds(HALF, HALF)]
        return remote(half, half, gs.at[a, 3], gr.at[a, 3], zdev(3))

    def down(a, r, j):
        z = zat(j)
        return remote(
            kv.at[a, 0, z], kv.at[a, r, z], gs.at[a, 4 * r + j], gr.at[a, 4 * r + j], xdev(r)
        )

    def down_all(a, j, act):
        @pl.when(x < NX - 1)
        def _():
            act(down(a, 1, j))

        @pl.when((x < NX - 2) & (zat(j) >= zh))
        def _():
            act(down(a, 2, j))

    def from_above(a):
        for j in range(NZ):
            @pl.when(x > 0)
            def _():
                down(a, 1, j).wait_recv()

            @pl.when((x > 1) & (zat(j) >= zh))
            def _():
                down(a, 2, j).wait_recv()

    def start(copy):
        copy.start()

    def wait_send(copy):
        copy.wait_send()

    loads[0].wait()
    pl.semaphore_wait(barrier, 9)
    ring(0, 0).start()
    ring(0, 1).start()
    down_all(0, 0, start)

    loads[1].wait()
    loads[2].wait()
    kv[1, 0, zh] = dot(mem[...], w[...]).astype(BF)
    ring(1, 0).start()
    ring(1, 1).start()
    down_all(1, 0, start)

    loads[3].wait()
    loads[4].wait()
    loads[5].wait()
    for h in range(HEADS):
        qall[TOK * h : TOK * (h + 1), :] = q_in[:, HD * h : HD * (h + 1)]
        gall[TOK * h : TOK * (h + 1), :] = g_in[:, HD * h : HD * (h + 1)]
    pad = jnp.zeros((LANES - HEADS * TOK, HD), BF)
    qall[HEADS * TOK :, :] = pad
    gall[HEADS * TOK :, :] = pad
    qt[...] = qall[...].T
    gt[...] = gall[...].T

    doc_row = doc[...].astype(F32)
    pair = doc[:, pl.ds(pl.multiple_of(2 * TOK * (c // 2), 128), 2 * TOK)].astype(F32)
    doc_q = jnp.where(c % 2 == 0, pair[:, :TOK], pair[:, TOK:])
    first = jnp.zeros((1, TOK), F32)
    for d in range(1, 8):
        before = jnp.sum(jnp.where(doc_row < d, 1.0, 0.0), axis=1, keepdims=True)
        first = jnp.where(doc_q == d, before, first)
    own_pos = lax.broadcasted_iota(jnp.int32, (1, TOK), 1).astype(F32) + (c * TOK).astype(F32)
    lane_pad = LANES - HEADS * TOK
    q_first = jnp.concatenate([first] * HEADS + [jnp.zeros((1, lane_pad), F32)], axis=1)
    q_pos = jnp.concatenate([own_pos] * HEADS + [jnp.full((1, lane_pad), float(SEQ), F32)], axis=1)

    part[:, 0] = jnp.zeros((2, NZ, TOK, HD), BF)
    top[...] = jnp.full((8, LANES), NEG, F32)
    total[...] = jnp.zeros((8, LANES), F32)

    blocks = jnp.minimum(c, SPAN) + 1

    def slot(d):
        b = c - d
        return x - b // NZ, b % NZ

    def there(r, j):
        z = zat(j)
        return (z <= zh, x > 0, (x > 1) & (z >= zh))[r]

    def scores(r, j):
        z = zat(j)
        d = NZ * r + zh - z
        kb = kv[0, r, z]
        key_pos = lax.broadcasted_iota(jnp.int32, (TOK, CHUNK), 0).astype(F32) + (
            (c - d) * TOK
        ).astype(F32)
        for i in range(LANES // CHUNK):
            at = slice(CHUNK * i, CHUNK * (i + 1))
            s = dot(kb, qt[:, at])
            s = jnp.where((key_pos >= q_first[:, at]) & (key_pos <= q_pos[:, at]), s, NEG)
            sbuf[d, :, at] = s
            top[:, at] = jnp.maximum(top[:, at], jnp.max(s.reshape(TOK // 8, 8, CHUNK), axis=0))

    def by_arrival(i):
        return jnp.where(i == 2, 3, jnp.where(i == 3, 2, i))

    def own_scores(j, carry):
        @pl.when(there(0, j))
        def _():
            scores(0, j)

        return carry

    def far_scores(r):
        def step(i, carry):
            j = by_arrival(i)

            @pl.when(there(r, j))
            def _():
                down(0, r, j).wait_recv()
                scores(r, j)

            return carry

        return step

    ring(0, 0).wait_recv()
    ring(0, 2).start()
    ring(0, 1).wait_recv()
    ring(0, 3).start()
    down_all(0, 1, start)
    down_all(0, 3, start)
    ring(1, 0).wait_recv()
    ring(1, 2).start()
    ring(1, 1).wait_recv()
    ring(1, 3).start()
    down_all(1, 1, start)
    down_all(1, 3, start)
    ring(0, 2).wait_recv()
    ring(0, 3).wait_recv()
    down_all(0, 2, start)
    lax.fori_loop(0, NZ, own_scores, 0)
    ring(1, 2).wait_recv()
    ring(1, 3).wait_recv()
    down_all(1, 2, start)
    lax.fori_loop(0, NZ, far_scores(1), 0)
    lax.fori_loop(0, NZ, far_scores(2), 0)

    top_row = jnp.max(top[...], axis=0, keepdims=True) * (SCALE * LOG2E)

    def numerators(d, carry):
        for i in range(LANES // CHUNK):
            at = slice(CHUNK * i, CHUNK * (i + 1))
            e = jnp.exp2(sbuf[d, :, at] * (SCALE * LOG2E) - top_row[:, at])
            sbuf[d, :, at] = e
            pbuf[d, :, at] = e.astype(BF)
            total[:, at] += jnp.sum(e.reshape(TOK // 8, 8, CHUNK), axis=0)
        return carry

    lax.fori_loop(0, blocks, numerators, 0)
    inv = 1.0 / jnp.sum(total[...], axis=0, keepdims=True)
    inv_col = jnp.broadcast_to(inv, (HD, LANES)).T
    gnorm[...] = (gall[...].astype(F32) * inv_col).astype(BF)

    def up(a, r, j):
        z = zat(j)
        return remote(
            part.at[a, r, z], from_x.at[a, r - 1, z], xs.at[a, 4 * (r - 1) + j],
            xr.at[a, 4 * (r - 1) + j], xdev(NX - r),
        )

    def up_all(a, act):
        for j in range(NZ):
            @pl.when(x > 0)
            def _():
                act(up(a, 1, j))

            @pl.when((x > 1) & (zat(j) >= zh))
            def _():
                act(up(a, 2, j))

    def over(a, j):
        return remote(zsend.at[a, zat(j)], from_z.at[a, j], zs.at[a, j], zr.at[a, j], zdev(j))

    def sum_rows(a):
        for j in (2, 1, 3, 0):
            z = zat(j)
            acc[...] = part[a, 0, z].astype(F32)

            @pl.when(x < NX - 1)
            def _():
                up(a, 1, j).wait_recv()
                acc[...] += from_x[a, 0, z].astype(F32)

            @pl.when((x < NX - 2) & (z >= zh))
            def _():
                up(a, 2, j).wait_recv()
                acc[...] += from_x[a, 1, z].astype(F32)

            if j:
                zsend[a, z] = acc[...].astype(BF)
                over(a, j).start()
            else:
                part[a, 0, z] = acc[...].astype(BF)

    def sum_ring(a):
        out = part[a, 0, zh].astype(F32)
        for j in (1, 3, 2):
            over(a, j).wait_recv()
            out = out + from_z[a, j].astype(F32)
        return out.astype(BF)

    def value_parts(r):
        def step(j, carry):
            z = zat(j)

            @pl.when(there(r, j))
            def _():
                part[1, r, z] = dot(pbuf[NZ * r + zh - z], gnorm[...]).astype(BF)
                if r:
                    up(1, r, j).start()

            return carry

        return step

    for r in (2, 1, 0):
        lax.fori_loop(0, NZ, value_parts(r), 0)

    from_above(1)
    ot[...] = jnp.zeros((HD, LANES), F32)

    def attend(d, carry):
        r, z = slot(d)
        ot[...] += dot(kv[1, r, z].T, pbuf[d])
        return carry

    lax.fori_loop(0, blocks, attend, 0)
    att = (ot[...] * inv).astype(BF).astype(F32)
    delta = jnp.sum(att * gt[...].astype(F32), axis=0, keepdims=True)
    att_rows = att.T.astype(BF)
    for h in range(HEADS):
        out_rows[:, HD * h : HD * (h + 1)] = att_rows[TOK * h : TOK * (h + 1), :]
    store_att = pltpu.make_async_copy(out_rows, att_hbm.at[0], lsem.at[6])
    store_att.start()

    sum_rows(1)

    dqt[...] = jnp.zeros((HD, LANES), F32)
    inv_scaled = inv * SCALE

    def grads(r, j):
        z = zat(j)
        d = NZ * r + zh - z
        vb = kv[1, r, z]
        kt = kv[0, r, z].T
        for i in range(LANES // CHUNK):
            at = slice(CHUNK * i, CHUNK * (i + 1))
            dprob = dot(vb, gt[:, at])
            pbuf[d, :, at] = (sbuf[d, :, at] * ((dprob - delta[:, at]) * inv_scaled[:, at])).astype(BF)
        part[0, r, z] = dot(pbuf[d], qall[...]).astype(BF)
        dqt[...] += dot(kt, pbuf[d])

    def grad_parts(r):
        def step(j, carry):
            @pl.when(there(r, j))
            def _():
                grads(r, j)
                if r:
                    up(0, r, j).start()

            return carry

        return step

    for r in (2, 1, 0):
        lax.fori_loop(0, NZ, grad_parts(r), 0)
    dq_rows = dqt[...].T.astype(BF)
    for h in range(HEADS):
        grad_rows[:, HD * h : HD * (h + 1)] = dq_rows[TOK * h : TOK * (h + 1), :]
    store_gq = pltpu.make_async_copy(grad_rows, gq_hbm.at[0], lsem.at[7])
    store_gq.start()

    memt[...] = mem[...].T
    dv[...] = sum_ring(1)

    def wx(k, o):
        return remote(wsend.at[k, o], wrecv.at[k, o], ws.at[k, o], wr.at[k, o], xdev(o))

    def wd(k):
        return remote(dsend.at[k], drecv.at[k], ds.at[k], dr.at[k], dpdev(k + 1))

    def wh(o):
        return remote(hsend.at[o], hrecv.at[o], hs.at[o], hr.at[o], zdev(o))

    for k in range(NDP):
        for o in (2, 1, 3, 0):
            row = NX * ROWS_X * lax.rem(dp + 1 + k, NDP) + ROWS_X * lax.rem(x + o, NX)
            piece = dot(memt[pl.ds(pl.multiple_of(row, 64), ROWS_X), :], dv[...])
            if o:
                wsend[k, o] = piece.astype(BF)
                wx(k, o).start()
            else:
                wown[k] = piece

    sum_rows(0)

    for k in range(NDP):
        piece = wown[k]
        for o in (1, 3, 2):
            wx(k, o).wait_recv()
            piece = piece + wrecv[k, o].astype(F32)
        if k < NDP - 1:
            dsend[k] = piece.astype(BF)
            wd(k).start()
        else:
            dacc[...] = piece
    for k in range(NDP - 1):
        wd(k).wait_recv()
        dacc[...] += drecv[k].astype(F32)
    for o in (2, 1, 3):
        rows = pl.ds(pl.multiple_of(ROWS_OUT * zat(o), 16), ROWS_OUT)
        hsend[o] = dacc[rows, :].astype(BF)
        wh(o).start()
    gk_out[...] = sum_ring(0)
    store_gk = pltpu.make_async_copy(gk_out, gk_hbm.at[0], lsem.at[8])
    store_gk.start()

    out = dacc[pl.ds(pl.multiple_of(ROWS_OUT * zh, 16), ROWS_OUT), :]
    for o in (1, 3, 2):
        wh(o).wait_recv()
        out = out + hrecv[o].astype(F32)
    gw_out[...] = out
    store_gw = pltpu.make_async_copy(gw_out, gw_hbm, lsem.at[9])
    store_gw.start()

    for a in range(2):
        for i in range(4):
            ring(a, i).wait_send()
        for j in range(NZ):
            down_all(a, j, wait_send)
        up_all(a, wait_send)
        for j in range(1, NZ):
            over(a, j).wait_send()
    for k in range(NDP):
        for o in range(1, NX):
            wx(k, o).wait_send()
    for k in range(NDP - 1):
        wd(k).wait_send()
    for o in range(1, NZ):
        wh(o).wait_send()
    for store in (store_att, store_gq, store_gk, store_gw):
        store.wait()


def hand_over(*refs):
    into = [pltpu.make_async_copy(refs[i], refs[8 + i], refs[12].at[i]) for i in range(4)]
    back = [pltpu.make_async_copy(refs[8 + i], refs[4 + i], refs[13].at[i]) for i in range(4)]
    for copy in into:
        copy.start()
    for i in range(4):
        into[i].wait()
        back[i].start()
    for copy in back:
        copy.wait()


def on_device(queries, keys, memory, value_weight, doc_ids, out_grad):
    vmem = pltpu.VMEM
    dma = pltpu.SemaphoreType.DMA
    anywhere = pl.BlockSpec(memory_space=pl.ANY)
    shape = jax.ShapeDtypeStruct
    outs = pl.pallas_call(
        kernel,
        out_shape=(
            shape((1, TOK, HEADS * HD), BF),
            shape((1, TOK, HEADS * HD), BF),
            shape((1, TOK, HD), BF),
            shape((ROWS_OUT, HD), F32),
        ),
        in_specs=[pl.BlockSpec(memory_space=pltpu.HBM)] * 6,
        out_specs=(anywhere,) * 4,
        scratch_shapes=[
            vmem((TOK, HEADS * HD), BF),
            vmem((TOK, HEADS * HD), BF),
            vmem((TOK, D), BF),
            vmem((D, HD), BF),
            vmem((1, SEQ), jnp.int32),
            vmem((2, 3, NZ, TOK, HD), BF),
            vmem((LANES, HD), BF),
            vmem((LANES, HD), BF),
            vmem((LANES, HD), BF),
            vmem((HD, LANES), BF),
            vmem((HD, LANES), BF),
            vmem((D, TOK), BF),
            vmem((SPAN + 1, TOK, LANES), F32),
            vmem((SPAN + 1, TOK, LANES), BF),
            vmem((8, LANES), F32),
            vmem((8, LANES), F32),
            vmem((HD, LANES), F32),
            vmem((HD, LANES), F32),
            vmem((TOK, HEADS * HD), BF),
            vmem((TOK, HEADS * HD), BF),
            vmem((2, 3, NZ, TOK, HD), BF),
            vmem((2, 2, NZ, TOK, HD), BF),
            vmem((TOK, HD), F32),
            vmem((2, NZ, TOK, HD), BF),
            vmem((2, NZ, TOK, HD), BF),
            vmem((TOK, HD), BF),
            vmem((TOK, HD), BF),
            vmem((NDP, NX, ROWS_X, HD), BF),
            vmem((NDP, ROWS_X, HD), F32),
            vmem((NDP, NX, ROWS_X, HD), BF),
            vmem((NDP, ROWS_X, HD), BF),
            vmem((ROWS_X, HD), F32),
            vmem((NDP, ROWS_X, HD), BF),
            vmem((NZ, ROWS_OUT, HD), BF),
            vmem((NZ, ROWS_OUT, HD), BF),
            vmem((ROWS_OUT, HD), F32),
            dma((10,)),
            dma((2, 12)), dma((2, 12)),
            dma((2, 8)), dma((2, 8)),
            dma((2, NZ)), dma((2, NZ)),
            dma((NDP, NX)), dma((NDP, NX)),
            dma((NDP,)), dma((NDP,)),
            dma((NZ,)), dma((NZ,)),
        ],
        compiler_params=pltpu.CompilerParams(
            collective_id=0, has_side_effects=True, vmem_limit_bytes=60 << 20
        ),
        name="cross_attention",
    )(queries, keys, memory, value_weight, doc_ids, out_grad)
    return pl.pallas_call(
        hand_over,
        out_shape=tuple(shape(o.shape, o.dtype) for o in outs),
        in_specs=[anywhere] * 4,
        out_specs=(anywhere,) * 4,
        scratch_shapes=[*(vmem(o.shape, o.dtype) for o in outs), dma((4,)), dma((4,))],
        compiler_params=pltpu.CompilerParams(vmem_limit_bytes=60 << 20),
        name="hand_over",
    )(*outs)


def solution(mesh):
    in_specs = (
        P("dp", "context", "tensor"),
        P("dp", "context", "tensor"),
        P("dp", "context", None),
        P(None, "tensor"),
        P("dp", None),
        P("dp", "context", "tensor"),
    )
    out_specs = (
        P("dp", "context", "tensor"),
        P("dp", "context", "tensor"),
        P("dp", "context", "tensor"),
        P(("dp", "context"), "tensor"),
    )
    return jax.shard_map(
        on_device, mesh=mesh, in_specs=in_specs, out_specs=out_specs, check_vma=False
    )
```

```python
import math

import jax
import jax.numpy as jnp
from jax import lax
from jax.experimental import pallas as pl
from jax.experimental.pallas import tpu as pltpu
from jax.sharding import PartitionSpec as P

MESH = pl.DeviceIdType.MESH
BF = jnp.bfloat16
F32 = jnp.float32

HD = 128
TOK = 192
HALF = TOK // 2
HEADS = 5
D = 5120
SEQ = 3072
NX = 4
NZ = 4
NDP = 4
SPAN = 8
BLOCKS = SPAN + 1
SLOTS = BLOCKS + NZ - 1
GROUP = 3
LANES = 1024
CHUNK = 256
ROWS_X = D // (NDP * NX)
ROWS_OUT = ROWS_X // NZ
SCALE = HD ** (-0.5)
LOG2E = math.log2(math.e)
NEG = -1e30


def dot(a, b):
    return jnp.dot(a, b, preferred_element_type=F32)


def dot_rows(a, b):
    return lax.dot_general(a, b, (((0,), (0,)), ((), ())), preferred_element_type=F32)


def remote(src, dst, send, recv, device):
    return pltpu.make_async_remote_copy(
        src_ref=src, dst_ref=dst, send_sem=send, recv_sem=recv, device_id=device, device_id_type=MESH
    )


def kernel(
    q_hbm, k_hbm, mem_hbm, w_hbm, doc_hbm, g_hbm,
    att_hbm, gq_hbm, gk_hbm, gw_hbm,
    q_in, g_in, mem, w, doc,
    kv, qall, gall, gnorm, qt, gt, memt,
    sbuf, pbuf, top, total, ot, dqt, out_rows, grad_rows,
    part, from_x, acc, zown, zsend, from_z, gk_out, dv,
    wsend, wown, wrecv, dsend, dacc, drecv, hsend, hrecv, gw_out,
    lsem, cs, cr, gs, gr, xs, xr, zs, zr, ws, wr, ds, dr, hs, hr,
):
    c = lax.axis_index("context")
    dp = lax.axis_index("dp")
    x = c // NZ
    zh = c % NZ

    def zat(j):
        return lax.rem(zh + j, NZ)

    def zdev(j):
        return {"context": x * NZ + zat(j)}

    def xdev(j):
        return {"context": lax.rem(c + NZ * j, NX * NZ)}

    def dpdev(j):
        return {"dp": lax.rem(dp + j, NDP)}

    loads = [
        pltpu.make_async_copy(k_hbm.at[0], kv.at[0, 0], lsem.at[0]),
        pltpu.make_async_copy(mem_hbm.at[0], mem, lsem.at[1]),
        pltpu.make_async_copy(w_hbm, w, lsem.at[2]),
        pltpu.make_async_copy(q_hbm.at[0], q_in, lsem.at[3]),
        pltpu.make_async_copy(g_hbm.at[0], g_in, lsem.at[4]),
        pltpu.make_async_copy(doc_hbm, doc, lsem.at[5]),
    ]
    for load in loads:
        load.start()

    barrier = pltpu.get_barrier_semaphore()
    for j in range(1, 4):
        for device in (zdev(j), xdev(j), dpdev(j)):
            pl.semaphore_signal(barrier, inc=1, device_id=device, device_id_type=MESH)

    def slot(z, h):
        e = h - z
        return jnp.where(e < 0, e + SLOTS, e)

    def ring(a, i):
        to = (1, 3)[i % 2]
        z = (zh, zh, zat(3), zat(1))[i]
        rows = (pl.ds(0, TOK), pl.ds(0, TOK), pl.ds(0, HALF), pl.ds(HALF, HALF))[i]
        return remote(
            kv.at[a, slot(z, zh), rows], kv.at[a, slot(z, zat(to)), rows],
            cs.at[a, i], cr.at[a, i], zdev(to),
        )

    def down(a, r, j):
        z = zat(j)
        d = NZ * r + zh - z
        return remote(kv.at[a, slot(z, zh)], kv.at[a, d], gs.at[a, d], gr.at[a, d], xdev(r))

    def down_all(a, j, act):
        @pl.when(x < NX - 1)
        def _():
            act(down(a, 1, j))

        @pl.when((x < NX - 2) & (zat(j) >= zh))
        def _():
            act(down(a, 2, j))

    def from_above(a, d):
        if d:
            @pl.when((d > zh) & (d <= c))
            def _():
                remote(kv.at[a, d], kv.at[a, d], gs.at[a, d], gr.at[a, d], xdev(1)).wait_recv()

    def start(copy):
        copy.start()

    def wait_send(copy):
        copy.wait_send()

    loads[0].wait()
    pl.semaphore_wait(barrier, 9)
    ring(0, 0).start()
    ring(0, 1).start()
    down_all(0, 0, start)

    loads[1].wait()
    loads[2].wait()
    kv[1, 0] = dot(mem[...], w[...]).astype(BF)
    ring(1, 0).start()
    ring(1, 1).start()
    down_all(1, 0, start)

    loads[3].wait()
    loads[4].wait()
    loads[5].wait()
    for h in range(HEADS):
        qall[TOK * h : TOK * (h + 1), :] = q_in[:, HD * h : HD * (h + 1)]
        gall[TOK * h : TOK * (h + 1), :] = g_in[:, HD * h : HD * (h + 1)]
    pad = jnp.zeros((LANES - HEADS * TOK, HD), BF)
    qall[HEADS * TOK :, :] = pad
    gall[HEADS * TOK :, :] = pad
    qt[...] = qall[...].T
    gt[...] = gall[...].T

    doc_row = doc[...].astype(F32)
    pair = doc[:, pl.ds(pl.multiple_of(2 * TOK * (c // 2), 128), 2 * TOK)].astype(F32)
    doc_q = jnp.where(c % 2 == 0, pair[:, :TOK], pair[:, TOK:])
    first = jnp.zeros((1, TOK), F32)
    for d in range(1, 8):
        before = jnp.sum(jnp.where(doc_row < d, 1.0, 0.0), axis=1, keepdims=True)
        first = jnp.where(doc_q == d, before, first)
    own_pos = lax.broadcasted_iota(jnp.int32, (1, TOK), 1).astype(F32) + (c * TOK).astype(F32)
    lane_pad = LANES - HEADS * TOK
    q_first = jnp.concatenate([first] * HEADS + [jnp.zeros((1, lane_pad), F32)], axis=1)
    q_pos = jnp.concatenate([own_pos] * HEADS + [jnp.full((1, lane_pad), float(SEQ), F32)], axis=1)

    top[...] = jnp.full((8, LANES), NEG, F32)
    total[...] = jnp.zeros((8, LANES), F32)

    for d in range(1, BLOCKS):
        @pl.when(d > c)
        def _():
            kv[:, d] = jnp.zeros((2, TOK, HD), BF)

    def scores(d):
        kb = kv[0, d]
        key_pos = lax.broadcasted_iota(jnp.int32, (TOK, CHUNK), 0).astype(F32) + (
            (c - d) * TOK
        ).astype(F32)
        rows = slice(TOK * d, TOK * (d + 1))
        for i in range(LANES // CHUNK):
            at = slice(CHUNK * i, CHUNK * (i + 1))
            s = dot(kb, qt[:, at])
            s = jnp.where((key_pos >= q_first[:, at]) & (key_pos <= q_pos[:, at]), s, NEG)
            sbuf[rows, at] = s
            top[:, at] = jnp.maximum(top[:, at], jnp.max(s.reshape(TOK // 8, 8, CHUNK), axis=0))

    ring(0, 0).wait_recv()
    ring(0, 2).start()
    ring(0, 1).wait_recv()
    ring(0, 3).start()
    down_all(0, 1, start)
    down_all(0, 3, start)
    ring(1, 0).wait_recv()
    ring(1, 2).start()
    ring(1, 1).wait_recv()
    ring(1, 3).start()
    down_all(1, 1, start)
    down_all(1, 3, start)
    ring(0, 2).wait_recv()
    ring(0, 3).wait_recv()
    down_all(0, 2, start)
    scores(0)
    ring(1, 2).wait_recv()
    ring(1, 3).wait_recv()
    down_all(1, 2, start)
    for d in (4, 8, 1, 3, 5, 7, 2, 6):
        from_above(0, d)
        scores(d)

    top_row = jnp.max(top[...], axis=0, keepdims=True) * (SCALE * LOG2E)

    def numerators(d, carry):
        rows = pl.ds(pl.multiple_of(TOK * d, TOK), TOK)
        for i in range(LANES // CHUNK):
            at = slice(CHUNK * i, CHUNK * (i + 1))
            e = jnp.exp2(sbuf[rows, at] * (SCALE * LOG2E) - top_row[:, at])
            sbuf[rows, at] = e
            pbuf[rows, at] = e.astype(BF)
            total[:, at] += jnp.sum(e.reshape(TOK // 8, 8, CHUNK), axis=0)
        return carry

    lax.fori_loop(0, BLOCKS, numerators, 0)
    inv = 1.0 / jnp.sum(total[...], axis=0, keepdims=True)
    inv_col = jnp.broadcast_to(inv, (HD, LANES)).T
    gnorm[...] = (gall[...].astype(F32) * inv_col).astype(BF)

    def up(a, d):
        r = jnp.where(d <= zh, 0, jnp.where(d <= zh + NZ, 1, 2))
        return remote(
            part.at[a, d], from_x.at[a, d], xs.at[a, d], xr.at[a, d],
            {"context": lax.rem(c - NZ * r + NX * NZ, NX * NZ)},
        )

    def up_if(a, d, act):
        if d:
            @pl.when((d > zh) & (d <= c))
            def _():
                act(up(a, d))

    def from_below(a, d):
        remote(part.at[a, d], from_x.at[a, d], xs.at[a, d], xr.at[a, d], xdev(1)).wait_recv()
        acc[...] += from_x[a, d].astype(F32)

    def over(a, j):
        return remote(zsend.at[a, zat(j)], from_z.at[a, j], zs.at[a, j], zr.at[a, j], zdev(j))

    def sum_rows(a):
        for j in (2, 1, 3, 0):
            z = zat(j)
            d = zh - z

            @pl.when(d >= 0)
            def _():
                acc[...] = part[a, d].astype(F32)

            @pl.when(d < 0)
            def _():
                acc[...] = jnp.zeros((TOK, HD), F32)

            @pl.when(x < NX - 1)
            def _():
                from_below(a, NZ + d)

            @pl.when((x < NX - 2) & (d <= 0))
            def _():
                from_below(a, 2 * NZ + d)

            if j:
                zsend[a, z] = acc[...].astype(BF)
                over(a, j).start()
            else:
                zown[a] = acc[...]

    def sum_ring(a):
        out = zown[a]
        for j in (1, 3, 2):
            over(a, j).wait_recv()
            out = out + from_z[a, j].astype(F32)
        return out.astype(BF)

    def group_rows(g):
        return slice(GROUP * TOK * g, GROUP * TOK * (g + 1))

    def put_parts(a, g, product):
        part[a, GROUP * g : GROUP * (g + 1)] = product.astype(BF).reshape(GROUP, TOK, HD)
        for d in reversed(range(GROUP * g, GROUP * (g + 1))):
            up_if(a, d, start)

    for g in (2, 1, 0):
        put_parts(1, g, dot(pbuf[group_rows(g), :], gnorm[...]))

    for d in range(1, BLOCKS):
        from_above(1, d)
    ot[...] = dot_rows(kv[1, :BLOCKS].reshape(BLOCKS * TOK, HD), pbuf[...])
    att = (ot[...] * inv).astype(BF).astype(F32)
    delta = jnp.sum(att * gt[...].astype(F32), axis=0, keepdims=True)
    att_rows = att.T.astype(BF)
    for h in range(HEADS):
        out_rows[:, HD * h : HD * (h + 1)] = att_rows[TOK * h : TOK * (h + 1), :]
    store_att = pltpu.make_async_copy(out_rows, att_hbm.at[0], lsem.at[6])
    store_att.start()

    sum_rows(1)

    inv_scaled = inv * SCALE

    def grads(g):
        vb = kv[1, GROUP * g : GROUP * (g + 1)].reshape(GROUP * TOK, HD)
        rows = group_rows(g)
        for i in range(LANES // CHUNK):
            at = slice(CHUNK * i, CHUNK * (i + 1))
            dprob = dot(vb, gt[:, at])
            pbuf[rows, at] = (sbuf[rows, at] * ((dprob - delta[:, at]) * inv_scaled[:, at])).astype(BF)
        put_parts(0, g, dot(pbuf[rows, :], qall[...]))

    for g in (2, 1, 0):
        grads(g)
    dqt[...] = dot_rows(kv[0, :BLOCKS].reshape(BLOCKS * TOK, HD), pbuf[...])
    dq_rows = dqt[...].T.astype(BF)
    for h in range(HEADS):
        grad_rows[:, HD * h : HD * (h + 1)] = dq_rows[TOK * h : TOK * (h + 1), :]
    store_gq = pltpu.make_async_copy(grad_rows, gq_hbm.at[0], lsem.at[7])
    store_gq.start()

    memt[...] = mem[...].T
    dv[...] = sum_ring(1)

    def wx(k, o):
        return remote(wsend.at[k, o], wrecv.at[k, o], ws.at[k, o], wr.at[k, o], xdev(o))

    def wd(k):
        return remote(dsend.at[k], drecv.at[k], ds.at[k], dr.at[k], dpdev(k + 1))

    def wh(o):
        return remote(hsend.at[o], hrecv.at[o], hs.at[o], hr.at[o], zdev(o))

    for k in range(NDP):
        for o in (2, 1, 3, 0):
            row = NX * ROWS_X * lax.rem(dp + 1 + k, NDP) + ROWS_X * lax.rem(x + o, NX)
            piece = dot(memt[pl.ds(pl.multiple_of(row, 64), ROWS_X), :], dv[...])
            if o:
                wsend[k, o] = piece.astype(BF)
                wx(k, o).start()
            else:
                wown[k] = piece

    sum_rows(0)

    for k in range(NDP):
        piece = wown[k]
        for o in (1, 3, 2):
            wx(k, o).wait_recv()
            piece = piece + wrecv[k, o].astype(F32)
        if k < NDP - 1:
            dsend[k] = piece.astype(BF)
            wd(k).start()
        else:
            dacc[...] = piece
    for k in range(NDP - 1):
        wd(k).wait_recv()
        dacc[...] += drecv[k].astype(F32)
    for o in (2, 1, 3):
        rows = pl.ds(pl.multiple_of(ROWS_OUT * zat(o), 16), ROWS_OUT)
        hsend[o] = dacc[rows, :].astype(BF)
        wh(o).start()
    gk_out[...] = sum_ring(0)
    store_gk = pltpu.make_async_copy(gk_out, gk_hbm.at[0], lsem.at[8])
    store_gk.start()

    out = dacc[pl.ds(pl.multiple_of(ROWS_OUT * zh, 16), ROWS_OUT), :]
    for o in (1, 3, 2):
        wh(o).wait_recv()
        out = out + hrecv[o].astype(F32)
    gw_out[...] = out
    store_gw = pltpu.make_async_copy(gw_out, gw_hbm, lsem.at[9])
    store_gw.start()

    for a in range(2):
        for i in range(4):
            ring(a, i).wait_send()
        for j in range(NZ):
            down_all(a, j, wait_send)
        for d in range(1, BLOCKS):
            up_if(a, d, wait_send)
        for j in range(1, NZ):
            over(a, j).wait_send()
    for k in range(NDP):
        for o in range(1, NX):
            wx(k, o).wait_send()
    for k in range(NDP - 1):
        wd(k).wait_send()
    for o in range(1, NZ):
        wh(o).wait_send()
    for store in (store_att, store_gq, store_gk, store_gw):
        store.wait()


def hand_over(*refs):
    into = [pltpu.make_async_copy(refs[i], refs[8 + i], refs[12].at[i]) for i in range(4)]
    back = [pltpu.make_async_copy(refs[8 + i], refs[4 + i], refs[13].at[i]) for i in range(4)]
    for copy in into:
        copy.start()
    for i in range(4):
        into[i].wait()
        back[i].start()
    for copy in back:
        copy.wait()


def on_device(queries, keys, memory, value_weight, doc_ids, out_grad):
    vmem = pltpu.VMEM
    dma = pltpu.SemaphoreType.DMA
    anywhere = pl.BlockSpec(memory_space=pl.ANY)
    shape = jax.ShapeDtypeStruct
    outs = pl.pallas_call(
        kernel,
        out_shape=(
            shape((1, TOK, HEADS * HD), BF),
            shape((1, TOK, HEADS * HD), BF),
            shape((1, TOK, HD), BF),
            shape((ROWS_OUT, HD), F32),
        ),
        in_specs=[pl.BlockSpec(memory_space=pltpu.HBM)] * 6,
        out_specs=(anywhere,) * 4,
        scratch_shapes=[
            vmem((TOK, HEADS * HD), BF),
            vmem((TOK, HEADS * HD), BF),
            vmem((TOK, D), BF),
            vmem((D, HD), BF),
            vmem((1, SEQ), jnp.int32),
            vmem((2, SLOTS, TOK, HD), BF),
            vmem((LANES, HD), BF),
            vmem((LANES, HD), BF),
            vmem((LANES, HD), BF),
            vmem((HD, LANES), BF),
            vmem((HD, LANES), BF),
            vmem((D, TOK), BF),
            vmem((BLOCKS * TOK, LANES), F32),
            vmem((BLOCKS * TOK, LANES), BF),
            vmem((8, LANES), F32),
            vmem((8, LANES), F32),
            vmem((HD, LANES), F32),
            vmem((HD, LANES), F32),
            vmem((TOK, HEADS * HD), BF),
            vmem((TOK, HEADS * HD), BF),
            vmem((2, BLOCKS, TOK, HD), BF),
            vmem((2, BLOCKS, TOK, HD), BF),
            vmem((TOK, HD), F32),
            vmem((2, TOK, HD), F32),
            vmem((2, NZ, TOK, HD), BF),
            vmem((2, NZ, TOK, HD), BF),
            vmem((TOK, HD), BF),
            vmem((TOK, HD), BF),
            vmem((NDP, NX, ROWS_X, HD), BF),
            vmem((NDP, ROWS_X, HD), F32),
            vmem((NDP, NX, ROWS_X, HD), BF),
            vmem((NDP, ROWS_X, HD), BF),
            vmem((ROWS_X, HD), F32),
            vmem((NDP, ROWS_X, HD), BF),
            vmem((NZ, ROWS_OUT, HD), BF),
            vmem((NZ, ROWS_OUT, HD), BF),
            vmem((ROWS_OUT, HD), F32),
            dma((10,)),
            dma((2, NZ)), dma((2, NZ)),
            dma((2, BLOCKS)), dma((2, BLOCKS)),
            dma((2, BLOCKS)), dma((2, BLOCKS)),
            dma((2, NZ)), dma((2, NZ)),
            dma((NDP, NX)), dma((NDP, NX)),
            dma((NDP,)), dma((NDP,)),
            dma((NZ,)), dma((NZ,)),
        ],
        compiler_params=pltpu.CompilerParams(
            collective_id=0, has_side_effects=True, vmem_limit_bytes=60 << 20
        ),
        name="cross_attention",
    )(queries, keys, memory, value_weight, doc_ids, out_grad)
    return pl.pallas_call(
        hand_over,
        out_shape=tuple(shape(o.shape, o.dtype) for o in outs),
        in_specs=[anywhere] * 4,
        out_specs=(anywhere,) * 4,
        scratch_shapes=[*(vmem(o.shape, o.dtype) for o in outs), dma((4,)), dma((4,))],
        compiler_params=pltpu.CompilerParams(vmem_limit_bytes=60 << 20),
        name="hand_over",
    )(*outs)


def solution(mesh):
    in_specs = (
        P("dp", "context", "tensor"),
        P("dp", "context", "tensor"),
        P("dp", "context", None),
        P(None, "tensor"),
        P("dp", None),
        P("dp", "context", "tensor"),
    )
    out_specs = (
        P("dp", "context", "tensor"),
        P("dp", "context", "tensor"),
        P("dp", "context", "tensor"),
        P(("dp", "context"), "tensor"),
    )
    return jax.shard_map(
        on_device, mesh=mesh, in_specs=in_specs, out_specs=out_specs, check_vma=False
    )
```

```python
import math

import jax
import jax.numpy as jnp
from jax import lax
from jax.experimental import pallas as pl
from jax.experimental.pallas import tpu as pltpu
from jax.sharding import PartitionSpec as P

MESH = pl.DeviceIdType.MESH
BF = jnp.bfloat16
F32 = jnp.float32

HD = 128
TOK = 192
HALF = TOK // 2
HEADS = 5
D = 5120
SEQ = 3072
NX = 4
NZ = 4
NDP = 4
NT = 8
SPAN = 8
BLOCKS = SPAN + 1
SLOTS = BLOCKS + NZ - 1
GROUP = 3
SENDS = ((2, 1), (3, 5, 8, 4), (6, 7))
LANES = 1024
CHUNK = 256
ROWS_X = D // (NDP * NX)
ROWS_OUT = ROWS_X // NZ
ROWS_T = NDP * ROWS_X // NT
SCALE = HD ** (-0.5)
LOG2E = math.log2(math.e)
NEG = -1e30


def dot(a, b):
    return jnp.dot(a, b, preferred_element_type=F32)


def dot_rows(a, b):
    return lax.dot_general(a, b, (((0,), (0,)), ((), ())), preferred_element_type=F32)


def remote(src, dst, send, recv, device):
    return pltpu.make_async_remote_copy(
        src_ref=src, dst_ref=dst, send_sem=send, recv_sem=recv, device_id=device, device_id_type=MESH
    )


def kernel(
    q_hbm, k_hbm, mem_hbm, w_hbm, doc_hbm, g_hbm,
    att_hbm, gq_hbm, gk_hbm, gw_hbm,
    q_in, g_in, mem, w, doc,
    kv, qall, gall, gnorm, qt, gt, memt,
    sbuf, pbuf, top, total, ot, dqt, out_rows, grad_rows,
    part, from_x, acc, zown, zsend, from_z, gk_out, dvx,
    mq, dsend, dacc, drecv, hsend, hrecv, gw_out,
    lsem, cs, cr, gs, gr, xs, xr, zs, zr, ms, mr, ns, nr, vs, vr, ds, dr, hs, hr,
):
    c = lax.axis_index("context")
    dp = lax.axis_index("dp")
    t = lax.axis_index("tensor")
    x = c // NZ
    zh = c % NZ

    def zat(j):
        return lax.rem(zh + j, NZ)

    def zdev(j):
        return {"context": x * NZ + zat(j)}

    def xdev(j):
        return {"context": lax.rem(c + NZ * j, NX * NZ)}

    def dpdev(j):
        return {"dp": lax.rem(dp + j, NDP)}

    def tdev(j):
        return {"tensor": lax.rem(t + j, NT)}

    loads = [
        pltpu.make_async_copy(k_hbm.at[0], kv.at[0, 0], lsem.at[0]),
        pltpu.make_async_copy(mem_hbm.at[0], mem, lsem.at[1]),
        pltpu.make_async_copy(w_hbm, w, lsem.at[2]),
        pltpu.make_async_copy(q_hbm.at[0], q_in, lsem.at[3]),
        pltpu.make_async_copy(g_hbm.at[0], g_in, lsem.at[4]),
        pltpu.make_async_copy(doc_hbm, doc, lsem.at[5]),
    ]
    for load in loads:
        load.start()

    barrier = pltpu.get_barrier_semaphore()
    for j in range(1, 4):
        for device in (zdev(j), xdev(j), dpdev(j)):
            pl.semaphore_signal(barrier, inc=1, device_id=device, device_id_type=MESH)
    for j in range(1, NT):
        pl.semaphore_signal(barrier, inc=1, device_id=tdev(j), device_id_type=MESH)

    def slot(z, h):
        e = h - z
        return jnp.where(e < 0, e + SLOTS, e)

    def ring(a, i):
        to = (1, 1, 3, 3, 1, 3)[i]
        z = (zh, zh, zh, zh, zat(3), zat(1))[i]
        rows = pl.ds((0, HALF, HALF, 0, 0, HALF)[i], HALF)
        return remote(
            kv.at[a, slot(z, zh), rows], kv.at[a, slot(z, zat(to)), rows],
            cs.at[a, i], cr.at[a, i], zdev(to),
        )

    def ring_start(a):
        for i in (0, 2, 1, 3):
            ring(a, i).start()

    def ring_forward(a):
        ring(a, 0).wait_recv()
        ring(a, 4).start()
        ring(a, 2).wait_recv()
        ring(a, 5).start()
        ring(a, 1).wait_recv()
        down_all(a, 3, start)
        ring(a, 3).wait_recv()
        down_all(a, 1, start)

    def ring_end(a):
        ring(a, 4).wait_recv()
        ring(a, 5).wait_recv()
        down_all(a, 2, start)

    def down(a, r, j):
        z = zat(j)
        d = NZ * r + zh - z
        return remote(kv.at[a, slot(z, zh)], kv.at[a, d], gs.at[a, d], gr.at[a, d], xdev(r))

    def down_all(a, j, act):
        @pl.when(x < NX - 1)
        def _():
            act(down(a, 1, j))

        @pl.when((x < NX - 2) & (zat(j) >= zh))
        def _():
            act(down(a, 2, j))

    def from_above(a, d):
        if d:
            @pl.when((d > zh) & (d <= c))
            def _():
                remote(kv.at[a, d], kv.at[a, d], gs.at[a, d], gr.at[a, d], xdev(1)).wait_recv()

    def start(copy):
        copy.start()

    def wait_send(copy):
        copy.wait_send()

    loads[0].wait()
    pl.semaphore_wait(barrier, 9 + NT - 1)
    ring_start(0)
    down_all(0, 0, start)

    loads[1].wait()
    loads[2].wait()
    kv[1, 0] = dot(mem[...], w[...]).astype(BF)
    ring_start(1)
    down_all(1, 0, start)

    def fetch(o):
        row = NX * ROWS_X * (t // 2) + ROWS_X * lax.rem(x + o, NX) + ROWS_T * (t % 2)
        return remote(
            memt.at[pl.ds(pl.multiple_of(row, 16), ROWS_T)], mq.at[o, t], ms.at[o], mr.at[o], xdev(o)
        )

    def share(o, k):
        return remote(mq.at[o, t], mq.at[o, t], ns.at[o, k], nr.at[o, k], tdev(k))

    memt[...] = mem[...].T
    for o in range(1, NX):
        fetch(o).start()

    loads[3].wait()
    loads[4].wait()
    loads[5].wait()
    for h in range(HEADS):
        qall[TOK * h : TOK * (h + 1), :] = q_in[:, HD * h : HD * (h + 1)]
        gall[TOK * h : TOK * (h + 1), :] = g_in[:, HD * h : HD * (h + 1)]
    pad = jnp.zeros((LANES - HEADS * TOK, HD), BF)
    qall[HEADS * TOK :, :] = pad
    gall[HEADS * TOK :, :] = pad
    qt[...] = qall[...].T
    gt[...] = gall[...].T

    doc_row = doc[...].astype(F32)
    pair = doc[:, pl.ds(pl.multiple_of(2 * TOK * (c // 2), 128), 2 * TOK)].astype(F32)
    doc_q = jnp.where(c % 2 == 0, pair[:, :TOK], pair[:, TOK:])
    first = jnp.zeros((1, TOK), F32)
    for d in range(1, 8):
        before = jnp.sum(jnp.where(doc_row < d, 1.0, 0.0), axis=1, keepdims=True)
        first = jnp.where(doc_q == d, before, first)
    own_pos = lax.broadcasted_iota(jnp.int32, (1, TOK), 1).astype(F32) + (c * TOK).astype(F32)
    lane_pad = LANES - HEADS * TOK
    q_first = jnp.concatenate([first] * HEADS + [jnp.zeros((1, lane_pad), F32)], axis=1)
    q_pos = jnp.concatenate([own_pos] * HEADS + [jnp.full((1, lane_pad), float(SEQ), F32)], axis=1)

    top[...] = jnp.full((8, LANES), NEG, F32)
    total[...] = jnp.zeros((8, LANES), F32)

    for d in range(1, BLOCKS):
        @pl.when(d > c)
        def _():
            kv[:, d] = jnp.zeros((2, TOK, HD), BF)

    def scores(d):
        kb = kv[0, d]
        key_pos = lax.broadcasted_iota(jnp.int32, (TOK, CHUNK), 0).astype(F32) + (
            (c - d) * TOK
        ).astype(F32)
        rows = slice(TOK * d, TOK * (d + 1))
        for i in range(LANES // CHUNK):
            at = slice(CHUNK * i, CHUNK * (i + 1))
            s = dot(kb, qt[:, at])
            s = jnp.where((key_pos >= q_first[:, at]) & (key_pos <= q_pos[:, at]), s, NEG)
            sbuf[rows, at] = s
            top[:, at] = jnp.maximum(top[:, at], jnp.max(s.reshape(TOK // 8, 8, CHUNK), axis=0))

    ring_forward(0)
    ring_forward(1)
    ring_end(0)
    for o in range(1, NX):
        fetch(o).wait_recv()
        for k in range(1, NT):
            share(o, k).start()
    scores(0)
    ring_end(1)
    for d in (4, 8, 1, 3, 5, 7, 2, 6):
        from_above(0, d)
        scores(d)

    top_row = jnp.max(top[...], axis=0, keepdims=True) * (SCALE * LOG2E)

    def numerators(d, carry):
        rows = pl.ds(pl.multiple_of(TOK * d, TOK), TOK)
        for i in range(LANES // CHUNK):
            at = slice(CHUNK * i, CHUNK * (i + 1))
            e = jnp.exp2(sbuf[rows, at] * (SCALE * LOG2E) - top_row[:, at])
            sbuf[rows, at] = e
            pbuf[rows, at] = e.astype(BF)
            total[:, at] += jnp.sum(e.reshape(TOK // 8, 8, CHUNK), axis=0)
        return carry

    lax.fori_loop(0, BLOCKS, numerators, 0)
    inv = 1.0 / jnp.sum(total[...], axis=0, keepdims=True)
    inv_col = jnp.broadcast_to(inv, (HD, LANES)).T
    gnorm[...] = (gall[...].astype(F32) * inv_col).astype(BF)

    def up(a, d):
        r = jnp.where(d <= zh, 0, jnp.where(d <= zh + NZ, 1, 2))
        return remote(
            part.at[a, d], from_x.at[a, d], xs.at[a, d], xr.at[a, d],
            {"context": lax.rem(c - NZ * r + NX * NZ, NX * NZ)},
        )

    def up_if(a, d, act):
        if d:
            @pl.when((d > zh) & (d <= c))
            def _():
                act(up(a, d))

    def from_below(a, d):
        remote(part.at[a, d], from_x.at[a, d], xs.at[a, d], xr.at[a, d], xdev(1)).wait_recv()
        acc[...] += from_x[a, d].astype(F32)

    def over(a, j):
        return remote(zsend.at[a, zat(j)], from_z.at[a, j], zs.at[a, j], zr.at[a, j], zdev(j))

    def sum_rows(a):
        for j in (2, 1, 3, 0):
            z = zat(j)
            d = zh - z

            @pl.when(d >= 0)
            def _():
                acc[...] = part[a, d].astype(F32)

            @pl.when(d < 0)
            def _():
                acc[...] = jnp.zeros((TOK, HD), F32)

            @pl.when(x < NX - 1)
            def _():
                from_below(a, NZ + d)

            @pl.when((x < NX - 2) & (d <= 0))
            def _():
                from_below(a, 2 * NZ + d)

            if j:
                zsend[a, z] = acc[...].astype(BF)
                over(a, j).start()
            else:
                zown[a] = acc[...]

    def sum_ring(a):
        out = zown[a]
        for j in (1, 3, 2):
            over(a, j).wait_recv()
            out = out + from_z[a, j].astype(F32)
        return out.astype(BF)

    def group_rows(g):
        return slice(GROUP * TOK * g, GROUP * TOK * (g + 1))

    def put_parts(a, g, product):
        part[a, GROUP * g : GROUP * (g + 1)] = product.astype(BF).reshape(GROUP, TOK, HD)
        for d in SENDS[g]:
            up_if(a, d, start)

    for g in (2, 0, 1):
        put_parts(1, g, dot(pbuf[group_rows(g), :], gnorm[...]))

    for d in range(1, BLOCKS):
        from_above(1, d)
    ot[...] = dot_rows(kv[1, :BLOCKS].reshape(BLOCKS * TOK, HD), pbuf[...])
    att = (ot[...] * inv).astype(BF).astype(F32)
    delta = jnp.sum(att * gt[...].astype(F32), axis=0, keepdims=True)
    att_rows = att.T.astype(BF)
    for h in range(HEADS):
        out_rows[:, HD * h : HD * (h + 1)] = att_rows[TOK * h : TOK * (h + 1), :]
    store_att = pltpu.make_async_copy(out_rows, att_hbm.at[0], lsem.at[6])
    store_att.start()

    sum_rows(1)

    inv_scaled = inv * SCALE

    def grads(g):
        vb = kv[1, GROUP * g : GROUP * (g + 1)].reshape(GROUP * TOK, HD)
        rows = group_rows(g)
        for i in range(LANES // CHUNK):
            at = slice(CHUNK * i, CHUNK * (i + 1))
            dprob = dot(vb, gt[:, at])
            pbuf[rows, at] = (sbuf[rows, at] * ((dprob - delta[:, at]) * inv_scaled[:, at])).astype(BF)
        put_parts(0, g, dot(pbuf[rows, :], qall[...]))

    for g in (2, 0, 1):
        grads(g)
    dqt[...] = dot_rows(kv[0, :BLOCKS].reshape(BLOCKS * TOK, HD), pbuf[...])
    dq_rows = dqt[...].T.astype(BF)
    for h in range(HEADS):
        grad_rows[:, HD * h : HD * (h + 1)] = dq_rows[TOK * h : TOK * (h + 1), :]
    store_gq = pltpu.make_async_copy(grad_rows, gq_hbm.at[0], lsem.at[7])
    store_gq.start()

    def spread(o):
        return remote(dvx.at[0], dvx.at[o], vs.at[o], vr.at[o], xdev(o))

    def wd(k):
        return remote(dsend.at[k], drecv.at[k], ds.at[k], dr.at[k], dpdev(k + 1))

    def wh(o):
        return remote(hsend.at[o], hrecv.at[o], hs.at[o], hr.at[o], zdev(o))

    dvx[0] = sum_ring(1)
    for o in range(1, NX):
        spread(o).start()
    sum_rows(0)

    for o in range(1, NX):
        for k in range(1, NT):
            share(o, k).wait_recv()
    for o in range(1, NX):
        spread(o).wait_recv()
    for k in range(NDP):
        to = lax.rem(dp + 1 + k, NDP)
        row = NX * ROWS_X * to + ROWS_X * x
        piece = dot(memt[pl.ds(pl.multiple_of(row, 64), ROWS_X), :], dvx[0])
        for o in range(1, NX):
            own = mq[o, pl.ds(2 * to, 2)].reshape(ROWS_X, TOK)
            piece = piece + dot(own, dvx[o])
        if k < NDP - 1:
            dsend[k] = piece.astype(BF)
            wd(k).start()
        else:
            dacc[...] = piece
    for k in range(NDP - 1):
        wd(k).wait_recv()
        dacc[...] += drecv[k].astype(F32)
    for o in (2, 1, 3):
        rows = pl.ds(pl.multiple_of(ROWS_OUT * zat(o), 16), ROWS_OUT)
        hsend[o] = dacc[rows, :].astype(BF)
        wh(o).start()
    gk_out[...] = sum_ring(0)
    store_gk = pltpu.make_async_copy(gk_out, gk_hbm.at[0], lsem.at[8])
    store_gk.start()

    out = dacc[pl.ds(pl.multiple_of(ROWS_OUT * zh, 16), ROWS_OUT), :]
    for o in (1, 3, 2):
        wh(o).wait_recv()
        out = out + hrecv[o].astype(F32)
    gw_out[...] = out
    store_gw = pltpu.make_async_copy(gw_out, gw_hbm, lsem.at[9])
    store_gw.start()

    for a in range(2):
        for i in range(6):
            ring(a, i).wait_send()
        for j in range(NZ):
            down_all(a, j, wait_send)
        for d in range(1, BLOCKS):
            up_if(a, d, wait_send)
        for j in range(1, NZ):
            over(a, j).wait_send()
    for o in range(1, NX):
        fetch(o).wait_send()
        spread(o).wait_send()
        for k in range(1, NT):
            share(o, k).wait_send()
    for k in range(NDP - 1):
        wd(k).wait_send()
    for o in range(1, NZ):
        wh(o).wait_send()
    for store in (store_att, store_gq, store_gk, store_gw):
        store.wait()


def hand_over(*refs):
    into = [pltpu.make_async_copy(refs[i], refs[8 + i], refs[12].at[i]) for i in range(4)]
    back = [pltpu.make_async_copy(refs[8 + i], refs[4 + i], refs[13].at[i]) for i in range(4)]
    for copy in into:
        copy.start()
    for i in range(4):
        into[i].wait()
        back[i].start()
    for copy in back:
        copy.wait()


def on_device(queries, keys, memory, value_weight, doc_ids, out_grad):
    vmem = pltpu.VMEM
    dma = pltpu.SemaphoreType.DMA
    anywhere = pl.BlockSpec(memory_space=pl.ANY)
    shape = jax.ShapeDtypeStruct
    outs = pl.pallas_call(
        kernel,
        out_shape=(
            shape((1, TOK, HEADS * HD), BF),
            shape((1, TOK, HEADS * HD), BF),
            shape((1, TOK, HD), BF),
            shape((ROWS_OUT, HD), F32),
        ),
        in_specs=[pl.BlockSpec(memory_space=pltpu.HBM)] * 6,
        out_specs=(anywhere,) * 4,
        scratch_shapes=[
            vmem((TOK, HEADS * HD), BF),
            vmem((TOK, HEADS * HD), BF),
            vmem((TOK, D), BF),
            vmem((D, HD), BF),
            vmem((1, SEQ), jnp.int32),
            vmem((2, SLOTS, TOK, HD), BF),
            vmem((LANES, HD), BF),
            vmem((LANES, HD), BF),
            vmem((LANES, HD), BF),
            vmem((HD, LANES), BF),
            vmem((HD, LANES), BF),
            vmem((D, TOK), BF),
            vmem((BLOCKS * TOK, LANES), F32),
            vmem((BLOCKS * TOK, LANES), BF),
            vmem((8, LANES), F32),
            vmem((8, LANES), F32),
            vmem((HD, LANES), F32),
            vmem((HD, LANES), F32),
            vmem((TOK, HEADS * HD), BF),
            vmem((TOK, HEADS * HD), BF),
            vmem((2, BLOCKS, TOK, HD), BF),
            vmem((2, BLOCKS, TOK, HD), BF),
            vmem((TOK, HD), F32),
            vmem((2, TOK, HD), F32),
            vmem((2, NZ, TOK, HD), BF),
            vmem((2, NZ, TOK, HD), BF),
            vmem((TOK, HD), BF),
            vmem((NX, TOK, HD), BF),
            vmem((NX, NT, ROWS_T, TOK), BF),
            vmem((NDP, ROWS_X, HD), BF),
            vmem((ROWS_X, HD), F32),
            vmem((NDP, ROWS_X, HD), BF),
            vmem((NZ, ROWS_OUT, HD), BF),
            vmem((NZ, ROWS_OUT, HD), BF),
            vmem((ROWS_OUT, HD), F32),
            dma((10,)),
            dma((2, 6)), dma((2, 6)),
            dma((2, BLOCKS)), dma((2, BLOCKS)),
            dma((2, BLOCKS)), dma((2, BLOCKS)),
            dma((2, NZ)), dma((2, NZ)),
            dma((NX,)), dma((NX,)),
            dma((NX, NT)), dma((NX, NT)),
            dma((NX,)), dma((NX,)),
            dma((NDP,)), dma((NDP,)),
            dma((NZ,)), dma((NZ,)),
        ],
        compiler_params=pltpu.CompilerParams(
            collective_id=0, has_side_effects=True, vmem_limit_bytes=60 << 20
        ),
        name="cross_attention",
    )(queries, keys, memory, value_weight, doc_ids, out_grad)
    return pl.pallas_call(
        hand_over,
        out_shape=tuple(shape(o.shape, o.dtype) for o in outs),
        in_specs=[anywhere] * 4,
        out_specs=(anywhere,) * 4,
        scratch_shapes=[*(vmem(o.shape, o.dtype) for o in outs), dma((4,)), dma((4,))],
        compiler_params=pltpu.CompilerParams(vmem_limit_bytes=60 << 20),
        name="hand_over",
    )(*outs)


def solution(mesh):
    in_specs = (
        P("dp", "context", "tensor"),
        P("dp", "context", "tensor"),
        P("dp", "context", None),
        P(None, "tensor"),
        P("dp", None),
        P("dp", "context", "tensor"),
    )
    out_specs = (
        P("dp", "context", "tensor"),
        P("dp", "context", "tensor"),
        P("dp", "context", "tensor"),
        P(("dp", "context"), "tensor"),
    )
    return jax.shard_map(
        on_device, mesh=mesh, in_specs=in_specs, out_specs=out_specs, check_vma=False
    )
```

```python
import math

import jax
import jax.numpy as jnp
from jax import lax
from jax.experimental import pallas as pl
from jax.experimental.pallas import tpu as pltpu
from jax.sharding import PartitionSpec as P

MESH = pl.DeviceIdType.MESH
BF = jnp.bfloat16
F32 = jnp.float32

HD = 128
TOK = 192
HALF = TOK // 2
HEADS = 5
D = 5120
SEQ = 3072
NX = 4
NZ = 4
NDP = 4
NT = 8
NRING = NDP * NZ
RELAYS = (2, -2, 6, -6)
SPAN = 8
BLOCKS = SPAN + 1
SLOTS = BLOCKS + NZ - 1
GROUP = 3
SENDS = ((2, 1), (3, 5, 8, 4), (6, 7))
LANES = 1024
CHUNK = 256
ROWS_X = D // (NDP * NX)
ROWS_OUT = ROWS_X // NZ
ROWS_T = NDP * ROWS_X // NT
SCALE = HD ** (-0.5)
LOG2E = math.log2(math.e)
NEG = -1e30


def dot(a, b):
    return jnp.dot(a, b, preferred_element_type=F32)


def dot_rows(a, b):
    return lax.dot_general(a, b, (((0,), (0,)), ((), ())), preferred_element_type=F32)


def remote(src, dst, send, recv, device):
    return pltpu.make_async_remote_copy(
        src_ref=src, dst_ref=dst, send_sem=send, recv_sem=recv, device_id=device, device_id_type=MESH
    )


def kernel(
    q_hbm, k_hbm, mem_hbm, w_hbm, doc_hbm, g_hbm,
    att_hbm, gq_hbm, gk_hbm, gw_hbm,
    q_in, g_in, mem, w, doc,
    kv, qall, gall, gnorm, qt, gt, memt,
    sbuf, pbuf, top, total, ot, dqt, out_rows, grad_rows,
    part, from_x, acc, zown, zsend, from_z, gk_out, dvx,
    mq, wacc, dsend, drecv, hsend, hrecv,
    lsem, cs, cr, gs, gr, xs, xr, zs, zr, ms, mr, ns, nr, vs, vr, ds, dr, hs, hr,
):
    c = lax.axis_index("context")
    dp = lax.axis_index("dp")
    t = lax.axis_index("tensor")
    x = c // NZ
    zh = c % NZ

    def zat(j):
        return lax.rem(zh + j, NZ)

    def zdev(j):
        return {"context": x * NZ + zat(j)}

    def xdev(j):
        return {"context": lax.rem(c + NZ * j, NX * NZ)}

    p = NDP * zh + dp

    def along(o):
        return lax.rem(p + o + NRING, NRING)

    def pdev(o):
        to = along(o)
        return {"dp": lax.rem(to, NDP), "context": x * NZ + to // NDP}

    def tdev(j):
        return {"tensor": lax.rem(t + j, NT)}

    loads = [
        pltpu.make_async_copy(k_hbm.at[0], kv.at[0, 0], lsem.at[0]),
        pltpu.make_async_copy(mem_hbm.at[0], mem, lsem.at[1]),
        pltpu.make_async_copy(w_hbm, w, lsem.at[2]),
        pltpu.make_async_copy(q_hbm.at[0], q_in, lsem.at[3]),
        pltpu.make_async_copy(g_hbm.at[0], g_in, lsem.at[4]),
        pltpu.make_async_copy(doc_hbm, doc, lsem.at[5]),
    ]
    for load in loads:
        load.start()

    barrier = pltpu.get_barrier_semaphore()
    for j in range(1, 4):
        for device in (zdev(j), xdev(j)):
            pl.semaphore_signal(barrier, inc=1, device_id=device, device_id_type=MESH)
    for o in (1, -1) + RELAYS:
        pl.semaphore_signal(barrier, inc=1, device_id=pdev(o), device_id_type=MESH)
    for j in range(1, NT):
        pl.semaphore_signal(barrier, inc=1, device_id=tdev(j), device_id_type=MESH)

    def slot(z, h):
        e = h - z
        return jnp.where(e < 0, e + SLOTS, e)

    def ring(a, i):
        to = (1, 1, 3, 3, 1, 3)[i]
        z = (zh, zh, zh, zh, zat(3), zat(1))[i]
        rows = pl.ds((0, HALF, HALF, 0, 0, HALF)[i], HALF)
        return remote(
            kv.at[a, slot(z, zh), rows], kv.at[a, slot(z, zat(to)), rows],
            cs.at[a, i], cr.at[a, i], zdev(to),
        )

    def ring_start(a):
        for i in (0, 2, 1, 3):
            ring(a, i).start()

    def ring_forward(a):
        ring(a, 0).wait_recv()
        ring(a, 4).start()
        ring(a, 2).wait_recv()
        ring(a, 5).start()
        ring(a, 1).wait_recv()
        down_all(a, 3, start)
        ring(a, 3).wait_recv()
        down_all(a, 1, start)

    def ring_end(a):
        ring(a, 4).wait_recv()
        ring(a, 5).wait_recv()
        down_all(a, 2, start)

    def down(a, r, j):
        z = zat(j)
        d = NZ * r + zh - z
        return remote(kv.at[a, slot(z, zh)], kv.at[a, d], gs.at[a, d], gr.at[a, d], xdev(r))

    def down_all(a, j, act):
        @pl.when(x < NX - 1)
        def _():
            act(down(a, 1, j))

        @pl.when((x < NX - 2) & (zat(j) >= zh))
        def _():
            act(down(a, 2, j))

    def from_above(a, d):
        if d:
            @pl.when((d > zh) & (d <= c))
            def _():
                remote(kv.at[a, d], kv.at[a, d], gs.at[a, d], gr.at[a, d], xdev(1)).wait_recv()

    def start(copy):
        copy.start()

    def wait_send(copy):
        copy.wait_send()

    loads[0].wait()
    pl.semaphore_wait(barrier, 6 + 6 + NT - 1)
    ring_start(0)
    down_all(0, 0, start)

    loads[1].wait()
    loads[2].wait()
    kv[1, 0] = dot(mem[...], w[...]).astype(BF)
    ring_start(1)
    down_all(1, 0, start)

    def fetch(o):
        row = NX * ROWS_X * (t // 2) + ROWS_X * lax.rem(x + o, NX) + ROWS_T * (t % 2)
        return remote(
            memt.at[pl.ds(pl.multiple_of(row, 16), ROWS_T)], mq.at[o, t], ms.at[o], mr.at[o], xdev(o)
        )

    def share(o, k):
        return remote(mq.at[o, t], mq.at[o, t], ns.at[o, k], nr.at[o, k], tdev(k))

    memt[...] = mem[...].T
    for o in range(1, NX):
        fetch(o).start()

    loads[3].wait()
    loads[4].wait()
    loads[5].wait()
    for h in range(HEADS):
        qall[TOK * h : TOK * (h + 1), :] = q_in[:, HD * h : HD * (h + 1)]
        gall[TOK * h : TOK * (h + 1), :] = g_in[:, HD * h : HD * (h + 1)]
    pad = jnp.zeros((LANES - HEADS * TOK, HD), BF)
    qall[HEADS * TOK :, :] = pad
    gall[HEADS * TOK :, :] = pad
    qt[...] = qall[...].T
    gt[...] = gall[...].T

    doc_row = doc[...].astype(F32)
    pair = doc[:, pl.ds(pl.multiple_of(2 * TOK * (c // 2), 128), 2 * TOK)].astype(F32)
    doc_q = jnp.where(c % 2 == 0, pair[:, :TOK], pair[:, TOK:])
    first = jnp.zeros((1, TOK), F32)
    for d in range(1, 8):
        before = jnp.sum(jnp.where(doc_row < d, 1.0, 0.0), axis=1, keepdims=True)
        first = jnp.where(doc_q == d, before, first)
    own_pos = lax.broadcasted_iota(jnp.int32, (1, TOK), 1).astype(F32) + (c * TOK).astype(F32)
    lane_pad = LANES - HEADS * TOK
    q_first = jnp.concatenate([first] * HEADS + [jnp.zeros((1, lane_pad), F32)], axis=1)
    q_pos = jnp.concatenate([own_pos] * HEADS + [jnp.full((1, lane_pad), float(SEQ), F32)], axis=1)

    top[...] = jnp.full((8, LANES), NEG, F32)
    total[...] = jnp.zeros((8, LANES), F32)

    for d in range(1, BLOCKS):
        @pl.when(d > c)
        def _():
            kv[:, d] = jnp.zeros((2, TOK, HD), BF)

    def scores(d):
        kb = kv[0, d]
        key_pos = lax.broadcasted_iota(jnp.int32, (TOK, CHUNK), 0).astype(F32) + (
            (c - d) * TOK
        ).astype(F32)
        rows = slice(TOK * d, TOK * (d + 1))
        for i in range(LANES // CHUNK):
            at = slice(CHUNK * i, CHUNK * (i + 1))
            s = dot(kb, qt[:, at])
            s = jnp.where((key_pos >= q_first[:, at]) & (key_pos <= q_pos[:, at]), s, NEG)
            sbuf[rows, at] = s
            top[:, at] = jnp.maximum(top[:, at], jnp.max(s.reshape(TOK // 8, 8, CHUNK), axis=0))

    ring_forward(0)
    ring_forward(1)
    ring_end(0)
    for o in range(1, NX):
        fetch(o).wait_recv()
        for k in range(1, NT):
            share(o, k).start()
    scores(0)
    ring_end(1)
    for d in (4, 8, 1, 3, 5, 7, 2, 6):
        from_above(0, d)
        scores(d)

    top_row = jnp.max(top[...], axis=0, keepdims=True) * (SCALE * LOG2E)

    def numerators(d, carry):
        rows = pl.ds(pl.multiple_of(TOK * d, TOK), TOK)
        for i in range(LANES // CHUNK):
            at = slice(CHUNK * i, CHUNK * (i + 1))
            e = jnp.exp2(sbuf[rows, at] * (SCALE * LOG2E) - top_row[:, at])
            sbuf[rows, at] = e
            pbuf[rows, at] = e.astype(BF)
            total[:, at] += jnp.sum(e.reshape(TOK // 8, 8, CHUNK), axis=0)
        return carry

    lax.fori_loop(0, BLOCKS, numerators, 0)
    inv = 1.0 / jnp.sum(total[...], axis=0, keepdims=True)
    inv_col = jnp.broadcast_to(inv, (HD, LANES)).T
    gnorm[...] = (gall[...].astype(F32) * inv_col).astype(BF)

    def up(a, d):
        r = jnp.where(d <= zh, 0, jnp.where(d <= zh + NZ, 1, 2))
        return remote(
            part.at[a, d], from_x.at[a, d], xs.at[a, d], xr.at[a, d],
            {"context": lax.rem(c - NZ * r + NX * NZ, NX * NZ)},
        )

    def up_if(a, d, act):
        if d:
            @pl.when((d > zh) & (d <= c))
            def _():
                act(up(a, d))

    def from_below(a, d):
        remote(part.at[a, d], from_x.at[a, d], xs.at[a, d], xr.at[a, d], xdev(1)).wait_recv()
        acc[...] += from_x[a, d].astype(F32)

    def over(a, j):
        return remote(zsend.at[a, zat(j)], from_z.at[a, j], zs.at[a, j], zr.at[a, j], zdev(j))

    def sum_rows(a):
        for j in (2, 1, 3, 0):
            z = zat(j)
            d = zh - z

            @pl.when(d >= 0)
            def _():
                acc[...] = part[a, d].astype(F32)

            @pl.when(d < 0)
            def _():
                acc[...] = jnp.zeros((TOK, HD), F32)

            @pl.when(x < NX - 1)
            def _():
                from_below(a, NZ + d)

            @pl.when((x < NX - 2) & (d <= 0))
            def _():
                from_below(a, 2 * NZ + d)

            if j:
                zsend[a, z] = acc[...].astype(BF)
                over(a, j).start()
            else:
                zown[a] = acc[...]

    def sum_ring(a):
        out = zown[a]
        for j in (1, 3, 2):
            over(a, j).wait_recv()
            out = out + from_z[a, j].astype(F32)
        return out.astype(BF)

    def group_rows(g):
        return slice(GROUP * TOK * g, GROUP * TOK * (g + 1))

    def put_parts(a, g, product):
        part[a, GROUP * g : GROUP * (g + 1)] = product.astype(BF).reshape(GROUP, TOK, HD)
        for d in SENDS[g]:
            up_if(a, d, start)

    for g in (2, 0, 1):
        put_parts(1, g, dot(pbuf[group_rows(g), :], gnorm[...]))

    sum_rows(1)

    for d in range(1, BLOCKS):
        from_above(1, d)
    ot[...] = dot_rows(kv[1, :BLOCKS].reshape(BLOCKS * TOK, HD), pbuf[...])
    att = (ot[...] * inv).astype(BF).astype(F32)
    delta = jnp.sum(att * gt[...].astype(F32), axis=0, keepdims=True)
    att_rows = att.T.astype(BF)
    for h in range(HEADS):
        out_rows[:, HD * h : HD * (h + 1)] = att_rows[TOK * h : TOK * (h + 1), :]
    store_att = pltpu.make_async_copy(out_rows, att_hbm.at[0], lsem.at[6])
    store_att.start()

    inv_scaled = inv * SCALE

    def grads(g):
        vb = kv[1, GROUP * g : GROUP * (g + 1)].reshape(GROUP * TOK, HD)
        rows = group_rows(g)
        for i in range(LANES // CHUNK):
            at = slice(CHUNK * i, CHUNK * (i + 1))
            dprob = dot(vb, gt[:, at])
            pbuf[rows, at] = (sbuf[rows, at] * ((dprob - delta[:, at]) * inv_scaled[:, at])).astype(BF)
        put_parts(0, g, dot(pbuf[rows, :], qall[...]))

    for g in (2, 0, 1):
        grads(g)
    dqt[...] = dot_rows(kv[0, :BLOCKS].reshape(BLOCKS * TOK, HD), pbuf[...])
    dq_rows = dqt[...].T.astype(BF)
    for h in range(HEADS):
        grad_rows[:, HD * h : HD * (h + 1)] = dq_rows[TOK * h : TOK * (h + 1), :]
    store_gq = pltpu.make_async_copy(grad_rows, gq_hbm.at[0], lsem.at[7])
    store_gq.start()

    def spread(o):
        return remote(dvx.at[0], dvx.at[o], vs.at[o], vr.at[o], xdev(o))

    side = 1 - 2 * lax.rem(t, 2)
    near = (-2 * side, side, -side)

    def wd(i):
        return remote(dsend.at[i], drecv.at[i], ds.at[i], dr.at[i], pdev(near[i]))

    def wh(i):
        return remote(hsend.at[i], hrecv.at[i], hs.at[i], hr.at[i], pdev(RELAYS[i]))

    def rows_of(o):
        to = along(o)
        row = ROWS_X * lax.rem(to, NDP) + ROWS_OUT * (to // NDP)
        return pl.ds(pl.multiple_of(row, 16), ROWS_OUT)

    dvx[0] = sum_ring(1)
    for o in range(1, NX):
        spread(o).start()
    sum_rows(0)

    for o in range(1, NX):
        for k in range(1, NT):
            share(o, k).wait_recv()
    for o in range(1, NX):
        spread(o).wait_recv()
    for k in range(NDP):
        rows = slice(ROWS_X * k, ROWS_X * (k + 1))
        row = NX * ROWS_X * k + ROWS_X * x
        piece = dot(memt[pl.ds(pl.multiple_of(row, 64), ROWS_X), :], dvx[0])
        for o in range(1, NX):
            piece = piece + dot(mq[o, 2 * k : 2 * k + 2].reshape(ROWS_X, TOK), dvx[o])
        wacc[rows, :] = piece
    for i in range(3):
        for e in range(4):
            dsend[i, e] = wacc[rows_of(near[i] + RELAYS[e]), :].astype(BF)
        wd(i).start()
    for i in range(3):
        wd(i).wait_recv()
    for e in (2, 3, 0, 1):
        piece = wacc[rows_of(RELAYS[e]), :]
        for i in range(3):
            piece = piece + drecv[i, e].astype(F32)
        hsend[e] = piece.astype(BF)
        wh(e).start()
    gk_out[...] = sum_ring(0)
    store_gk = pltpu.make_async_copy(gk_out, gk_hbm.at[0], lsem.at[8])
    store_gk.start()

    out = jnp.zeros((ROWS_OUT, HD), F32)
    for e in range(4):
        wh(e).wait_recv()
        out = out + hrecv[e].astype(F32)
    gw_hbm[...] = out

    for a in range(2):
        for i in range(6):
            ring(a, i).wait_send()
        for j in range(NZ):
            down_all(a, j, wait_send)
        for d in range(1, BLOCKS):
            up_if(a, d, wait_send)
        for j in range(1, NZ):
            over(a, j).wait_send()
    for o in range(1, NX):
        fetch(o).wait_send()
        spread(o).wait_send()
        for k in range(1, NT):
            share(o, k).wait_send()
    for i in range(3):
        wd(i).wait_send()
    for e in range(4):
        wh(e).wait_send()
    for store in (store_att, store_gq, store_gk):
        store.wait()


def hand_over(*refs):
    copies = [pltpu.make_async_copy(refs[i], refs[4 + i], refs[8].at[i]) for i in range(4)]
    for copy in copies:
        copy.start()
    for copy in copies:
        copy.wait()


def on_device(queries, keys, memory, value_weight, doc_ids, out_grad):
    vmem = pltpu.VMEM
    dma = pltpu.SemaphoreType.DMA
    anywhere = pl.BlockSpec(memory_space=pl.ANY)
    shape = jax.ShapeDtypeStruct
    outs = pl.pallas_call(
        kernel,
        out_shape=(
            shape((1, TOK, HEADS * HD), BF),
            shape((1, TOK, HEADS * HD), BF),
            shape((1, TOK, HD), BF),
            shape((ROWS_OUT, HD), F32),
        ),
        in_specs=[pl.BlockSpec(memory_space=pltpu.HBM)] * 6,
        out_specs=(pl.BlockSpec(memory_space=pltpu.VMEM),) * 4,
        scratch_shapes=[
            vmem((TOK, HEADS * HD), BF),
            vmem((TOK, HEADS * HD), BF),
            vmem((TOK, D), BF),
            vmem((D, HD), BF),
            vmem((1, SEQ), jnp.int32),
            vmem((2, SLOTS, TOK, HD), BF),
            vmem((LANES, HD), BF),
            vmem((LANES, HD), BF),
            vmem((LANES, HD), BF),
            vmem((HD, LANES), BF),
            vmem((HD, LANES), BF),
            vmem((D, TOK), BF),
            vmem((BLOCKS * TOK, LANES), F32),
            vmem((BLOCKS * TOK, LANES), BF),
            vmem((8, LANES), F32),
            vmem((8, LANES), F32),
            vmem((HD, LANES), F32),
            vmem((HD, LANES), F32),
            vmem((TOK, HEADS * HD), BF),
            vmem((TOK, HEADS * HD), BF),
            vmem((2, BLOCKS, TOK, HD), BF),
            vmem((2, BLOCKS, TOK, HD), BF),
            vmem((TOK, HD), F32),
            vmem((2, TOK, HD), F32),
            vmem((2, NZ, TOK, HD), BF),
            vmem((2, NZ, TOK, HD), BF),
            vmem((TOK, HD), BF),
            vmem((NX, TOK, HD), BF),
            vmem((NX, NT, ROWS_T, TOK), BF),
            vmem((NDP * ROWS_X, HD), F32),
            vmem((3, 4, ROWS_OUT, HD), BF),
            vmem((3, 4, ROWS_OUT, HD), BF),
            vmem((4, ROWS_OUT, HD), BF),
            vmem((4, ROWS_OUT, HD), BF),
            dma((10,)),
            dma((2, 6)), dma((2, 6)),
            dma((2, BLOCKS)), dma((2, BLOCKS)),
            dma((2, BLOCKS)), dma((2, BLOCKS)),
            dma((2, NZ)), dma((2, NZ)),
            dma((NX,)), dma((NX,)),
            dma((NX, NT)), dma((NX, NT)),
            dma((NX,)), dma((NX,)),
            dma((3,)), dma((3,)),
            dma((4,)), dma((4,)),
        ],
        compiler_params=pltpu.CompilerParams(
            collective_id=0, has_side_effects=True, vmem_limit_bytes=60 << 20
        ),
        name="cross_attention",
    )(queries, keys, memory, value_weight, doc_ids, out_grad)
    return pl.pallas_call(
        hand_over,
        out_shape=tuple(shape(o.shape, o.dtype) for o in outs),
        in_specs=[pl.BlockSpec(memory_space=pltpu.VMEM)] * 4,
        out_specs=(anywhere,) * 4,
        scratch_shapes=[dma((4,))],
        compiler_params=pltpu.CompilerParams(vmem_limit_bytes=60 << 20),
        name="hand_over",
    )(*outs)


def solution(mesh):
    in_specs = (
        P("dp", "context", "tensor"),
        P("dp", "context", "tensor"),
        P("dp", "context", None),
        P(None, "tensor"),
        P("dp", None),
        P("dp", "context", "tensor"),
    )
    out_specs = (
        P("dp", "context", "tensor"),
        P("dp", "context", "tensor"),
        P("dp", "context", "tensor"),
        P(("dp", "context"), "tensor"),
    )
    return jax.shard_map(
        on_device, mesh=mesh, in_specs=in_specs, out_specs=out_specs, check_vma=False
    )
```

```python
import math

import jax
import jax.numpy as jnp
from jax import lax
from jax.experimental import pallas as pl
from jax.experimental.pallas import tpu as pltpu
from jax.sharding import PartitionSpec as P

MESH = pl.DeviceIdType.MESH
BF = jnp.bfloat16
F32 = jnp.float32

HD = 128
TOK = 192
HALF = TOK // 2
HEADS = 5
D = 5120
SEQ = 3072
NX = 4
NZ = 4
NDP = 4
NT = 8
NRING = NDP * NZ
RELAYS = (2, -2, 6, -6)
SPAN = 8
BLOCKS = SPAN + 1
SLOTS = BLOCKS + NZ - 1
GROUP = 3
SENDS = ((2, 1), (3, 5, 8, 4), (6, 7))
LANES = 1024
CHUNK = 256
ROWS_X = D // (NDP * NX)
ROWS_OUT = ROWS_X // NZ
ROWS_T = NDP * ROWS_X // NT
SCALE = HD ** (-0.5)
LOG2E = math.log2(math.e)
NEG = -1e30


def dot(a, b):
    return jnp.dot(a, b, preferred_element_type=F32)


def dot_rows(a, b):
    return lax.dot_general(a, b, (((0,), (0,)), ((), ())), preferred_element_type=F32)


def remote(src, dst, send, recv, device):
    return pltpu.make_async_remote_copy(
        src_ref=src, dst_ref=dst, send_sem=send, recv_sem=recv, device_id=device, device_id_type=MESH
    )


def kernel(
    q_hbm, k_hbm, mem_hbm, w_hbm, doc_hbm, g_hbm,
    att_hbm, gq_hbm, gk_hbm, gw_hbm,
    q_in, g_in, mem, w, doc,
    kv, qall, gall, gnorm, qt, gt, memt,
    sbuf, pbuf, top, total, ot, dqt, out_rows, grad_rows,
    part, from_x, acc, zown, zsend, from_z, gk_out, dvx,
    mq, wacc, dsend, drecv, hsend, hrecv,
    lsem, cs, cr, gs, gr, xs, xr, zs, zr, ms, mr, ns, nr, vs, vr, ds, dr, hs, hr,
):
    c = lax.axis_index("context")
    dp = lax.axis_index("dp")
    t = lax.axis_index("tensor")
    x = c // NZ
    zh = c % NZ

    def zat(j):
        return lax.rem(zh + j, NZ)

    def zdev(j):
        return {"context": x * NZ + zat(j)}

    def xdev(j):
        return {"context": lax.rem(c + NZ * j, NX * NZ)}

    p = NDP * zh + dp

    def along(o):
        return lax.rem(p + o + NRING, NRING)

    def pdev(o):
        to = along(o)
        return {"dp": lax.rem(to, NDP), "context": x * NZ + to // NDP}

    def tdev(j):
        return {"tensor": lax.rem(t + j, NT)}

    loads = [
        pltpu.make_async_copy(k_hbm.at[0], kv.at[0, 0], lsem.at[0]),
        pltpu.make_async_copy(mem_hbm.at[0], mem, lsem.at[1]),
        pltpu.make_async_copy(w_hbm, w, lsem.at[2]),
        pltpu.make_async_copy(q_hbm.at[0], q_in, lsem.at[3]),
        pltpu.make_async_copy(g_hbm.at[0], g_in, lsem.at[4]),
        pltpu.make_async_copy(doc_hbm, doc, lsem.at[5]),
    ]
    for load in loads:
        load.start()

    barrier = pltpu.get_barrier_semaphore()
    for j in range(1, 4):
        for device in (zdev(j), xdev(j)):
            pl.semaphore_signal(barrier, inc=1, device_id=device, device_id_type=MESH)
    for o in (1, -1) + RELAYS:
        pl.semaphore_signal(barrier, inc=1, device_id=pdev(o), device_id_type=MESH)
    for j in range(1, NT):
        pl.semaphore_signal(barrier, inc=1, device_id=tdev(j), device_id_type=MESH)

    def slot(z, h):
        e = h - z
        return jnp.where(e < 0, e + SLOTS, e)

    def ring(a, i):
        to = (1, 1, 3, 3, 1, 3)[i]
        z = (zh, zh, zh, zh, zat(3), zat(1))[i]
        rows = pl.ds((0, HALF, HALF, 0, 0, HALF)[i], HALF)
        return remote(
            kv.at[a, slot(z, zh), rows], kv.at[a, slot(z, zat(to)), rows],
            cs.at[a, i], cr.at[a, i], zdev(to),
        )

    def ring_start(a):
        for i in (0, 2, 1, 3):
            ring(a, i).start()

    def ring_forward(a):
        ring(a, 0).wait_recv()
        ring(a, 4).start()
        ring(a, 2).wait_recv()
        ring(a, 5).start()
        ring(a, 1).wait_recv()
        down_all(a, 3, start)
        ring(a, 3).wait_recv()
        down_all(a, 1, start)

    def ring_end(a):
        ring(a, 4).wait_recv()
        ring(a, 5).wait_recv()
        down_all(a, 2, start)

    def down(a, r, j):
        z = zat(j)
        d = NZ * r + zh - z
        return remote(kv.at[a, slot(z, zh)], kv.at[a, d], gs.at[a, d], gr.at[a, d], xdev(r))

    def down_all(a, j, act):
        @pl.when(x < NX - 1)
        def _():
            act(down(a, 1, j))

        @pl.when((x < NX - 2) & (zat(j) >= zh))
        def _():
            act(down(a, 2, j))

    def from_above(a, d):
        if d:
            @pl.when((d > zh) & (d <= c))
            def _():
                remote(kv.at[a, d], kv.at[a, d], gs.at[a, d], gr.at[a, d], xdev(1)).wait_recv()

    def start(copy):
        copy.start()

    def wait_send(copy):
        copy.wait_send()

    loads[0].wait()
    pl.semaphore_wait(barrier, 6 + 6 + NT - 1)
    ring_start(0)
    down_all(0, 0, start)

    loads[1].wait()
    loads[2].wait()
    kv[1, 0] = dot(mem[...], w[...]).astype(BF)
    ring_start(1)
    down_all(1, 0, start)

    def fetch(o):
        row = NX * ROWS_X * (t // 2) + ROWS_X * lax.rem(x + o, NX) + ROWS_T * (t % 2)
        return remote(
            memt.at[pl.ds(pl.multiple_of(row, 16), ROWS_T)], mq.at[o, t], ms.at[o], mr.at[o], xdev(o)
        )

    def share(o, k):
        return remote(mq.at[o, t], mq.at[o, t], ns.at[o, k], nr.at[o, k], tdev(k))

    memt[...] = mem[...].T
    for o in range(1, NX):
        fetch(o).start()

    loads[3].wait()
    loads[4].wait()
    loads[5].wait()
    for h in range(HEADS):
        qall[TOK * h : TOK * (h + 1), :] = q_in[:, HD * h : HD * (h + 1)]
        gall[TOK * h : TOK * (h + 1), :] = g_in[:, HD * h : HD * (h + 1)]
    pad = jnp.zeros((LANES - HEADS * TOK, HD), BF)
    qall[HEADS * TOK :, :] = pad
    gall[HEADS * TOK :, :] = pad
    qt[...] = qall[...].T
    gt[...] = gall[...].T

    doc_row = doc[...].astype(F32)
    pair = doc[:, pl.ds(pl.multiple_of(2 * TOK * (c // 2), 128), 2 * TOK)].astype(F32)
    doc_q = jnp.where(c % 2 == 0, pair[:, :TOK], pair[:, TOK:])
    first = jnp.zeros((1, TOK), F32)
    for d in range(1, 8):
        before = jnp.sum(jnp.where(doc_row < d, 1.0, 0.0), axis=1, keepdims=True)
        first = jnp.where(doc_q == d, before, first)
    own_pos = lax.broadcasted_iota(jnp.int32, (1, TOK), 1).astype(F32) + (c * TOK).astype(F32)
    lane_pad = LANES - HEADS * TOK
    q_first = jnp.concatenate([first] * HEADS + [jnp.zeros((1, lane_pad), F32)], axis=1)
    q_pos = jnp.concatenate([own_pos] * HEADS + [jnp.full((1, lane_pad), float(SEQ), F32)], axis=1)

    top[...] = jnp.full((8, LANES), NEG, F32)
    total[...] = jnp.zeros((8, LANES), F32)

    for d in range(1, BLOCKS):
        @pl.when(d > c)
        def _():
            kv[:, d] = jnp.zeros((2, TOK, HD), BF)

    def scores(d):
        kb = kv[0, d]
        key_pos = lax.broadcasted_iota(jnp.int32, (TOK, CHUNK), 0).astype(F32) + (
            (c - d) * TOK
        ).astype(F32)
        rows = slice(TOK * d, TOK * (d + 1))
        for i in range(LANES // CHUNK):
            at = slice(CHUNK * i, CHUNK * (i + 1))
            s = dot(kb, qt[:, at])
            s = jnp.where((key_pos >= q_first[:, at]) & (key_pos <= q_pos[:, at]), s, NEG)
            sbuf[rows, at] = s
            top[:, at] = jnp.maximum(top[:, at], jnp.max(s.reshape(TOK // 8, 8, CHUNK), axis=0))

    ring_forward(0)
    ring_forward(1)
    ring_end(0)
    for o in range(1, NX):
        fetch(o).wait_recv()
        for k in range(1, NT):
            share(o, k).start()
    scores(0)
    ring_end(1)
    for d in (4, 8, 1, 3, 5, 7, 2, 6):
        from_above(0, d)
        scores(d)

    top_row = jnp.max(top[...], axis=0, keepdims=True) * (SCALE * LOG2E)

    def numerators(d, carry):
        rows = pl.ds(pl.multiple_of(TOK * d, TOK), TOK)
        for i in range(LANES // CHUNK):
            at = slice(CHUNK * i, CHUNK * (i + 1))
            e = jnp.exp2(sbuf[rows, at] * (SCALE * LOG2E) - top_row[:, at])
            sbuf[rows, at] = e
            pbuf[rows, at] = e.astype(BF)
            total[:, at] += jnp.sum(e.reshape(TOK // 8, 8, CHUNK), axis=0)
        return carry

    lax.fori_loop(0, BLOCKS, numerators, 0)
    inv = 1.0 / jnp.sum(total[...], axis=0, keepdims=True)
    inv_col = jnp.broadcast_to(inv, (HD, LANES)).T
    gnorm[...] = (gall[...].astype(F32) * inv_col).astype(BF)

    def up(a, d):
        r = jnp.where(d <= zh, 0, jnp.where(d <= zh + NZ, 1, 2))
        return remote(
            part.at[a, d], from_x.at[a, d], xs.at[a, d], xr.at[a, d],
            {"context": lax.rem(c - NZ * r + NX * NZ, NX * NZ)},
        )

    def up_if(a, d, act):
        if d:
            @pl.when((d > zh) & (d <= c))
            def _():
                act(up(a, d))

    def from_below(a, d):
        remote(part.at[a, d], from_x.at[a, d], xs.at[a, d], xr.at[a, d], xdev(1)).wait_recv()
        acc[...] += from_x[a, d].astype(F32)

    def over(a, j):
        return remote(zsend.at[a, zat(j)], from_z.at[a, j], zs.at[a, j], zr.at[a, j], zdev(j))

    def sum_rows(a):
        for j in (2, 1, 3, 0):
            z = zat(j)
            d = zh - z

            @pl.when(d >= 0)
            def _():
                acc[...] = part[a, d].astype(F32)

            @pl.when(d < 0)
            def _():
                acc[...] = jnp.zeros((TOK, HD), F32)

            @pl.when(x < NX - 1)
            def _():
                from_below(a, NZ + d)

            @pl.when((x < NX - 2) & (d <= 0))
            def _():
                from_below(a, 2 * NZ + d)

            if j:
                zsend[a, z] = acc[...].astype(BF)
                over(a, j).start()
            else:
                zown[a] = acc[...]

    def sum_ring(a):
        out = zown[a]
        for j in (1, 3, 2):
            over(a, j).wait_recv()
            out = out + from_z[a, j].astype(F32)
        return out.astype(BF)

    def group_rows(g):
        return slice(GROUP * TOK * g, GROUP * TOK * (g + 1))

    def put_parts(a, g, product):
        part[a, GROUP * g : GROUP * (g + 1)] = product.astype(BF).reshape(GROUP, TOK, HD)
        for d in SENDS[g]:
            up_if(a, d, start)

    for g in (2, 0, 1):
        put_parts(1, g, dot(pbuf[group_rows(g), :], gnorm[...]))

    sum_rows(1)

    for d in range(1, BLOCKS):
        from_above(1, d)
    ot[...] = dot_rows(kv[1, :BLOCKS].reshape(BLOCKS * TOK, HD), pbuf[...])
    att = (ot[...] * inv).astype(BF).astype(F32)
    delta = jnp.sum(att * gt[...].astype(F32), axis=0, keepdims=True)
    att_rows = att.T.astype(BF)
    for h in range(HEADS):
        out_rows[:, HD * h : HD * (h + 1)] = att_rows[TOK * h : TOK * (h + 1), :]
    store_att = pltpu.make_async_copy(out_rows, att_hbm.at[0], lsem.at[6])
    store_att.start()

    inv_scaled = inv * SCALE

    def grads(g):
        vb = kv[1, GROUP * g : GROUP * (g + 1)].reshape(GROUP * TOK, HD)
        rows = group_rows(g)
        for i in range(LANES // CHUNK):
            at = slice(CHUNK * i, CHUNK * (i + 1))
            dprob = dot(vb, gt[:, at])
            pbuf[rows, at] = (sbuf[rows, at] * ((dprob - delta[:, at]) * inv_scaled[:, at])).astype(BF)
        put_parts(0, g, dot(pbuf[rows, :], qall[...]))

    for g in (2, 0, 1):
        grads(g)

    def spread(o):
        return remote(dvx.at[0], dvx.at[o], vs.at[o], vr.at[o], xdev(o))

    side = 1 - 2 * lax.rem(t, 2)
    near = (-2 * side, side, -side)

    def wd(i):
        return remote(dsend.at[i], drecv.at[i], ds.at[i], dr.at[i], pdev(near[i]))

    def wh(i):
        return remote(hsend.at[i], hrecv.at[i], hs.at[i], hr.at[i], pdev(RELAYS[i]))

    def rows_of(o):
        to = along(o)
        row = ROWS_X * lax.rem(to, NDP) + ROWS_OUT * (to // NDP)
        return pl.ds(pl.multiple_of(row, 16), ROWS_OUT)

    dvx[0] = sum_ring(1)
    for o in range(1, NX):
        spread(o).start()
    sum_rows(0)

    dqt[...] = dot_rows(kv[0, :BLOCKS].reshape(BLOCKS * TOK, HD), pbuf[...])
    dq_rows = dqt[...].T.astype(BF)
    for h in range(HEADS):
        grad_rows[:, HD * h : HD * (h + 1)] = dq_rows[TOK * h : TOK * (h + 1), :]
    store_gq = pltpu.make_async_copy(grad_rows, gq_hbm.at[0], lsem.at[7])
    store_gq.start()
    for o in range(1, NX):
        for k in range(1, NT):
            share(o, k).wait_recv()
    for o in range(1, NX):
        spread(o).wait_recv()
    for k in range(NDP):
        rows = slice(ROWS_X * k, ROWS_X * (k + 1))
        row = NX * ROWS_X * k + ROWS_X * x
        piece = dot(memt[pl.ds(pl.multiple_of(row, 64), ROWS_X), :], dvx[0])
        for o in range(1, NX):
            piece = piece + dot(mq[o, 2 * k : 2 * k + 2].reshape(ROWS_X, TOK), dvx[o])
        wacc[rows, :] = piece
    for i in range(3):
        for e in range(4):
            dsend[i, e] = wacc[rows_of(near[i] + RELAYS[e]), :].astype(BF)
        wd(i).start()
    for i in range(3):
        wd(i).wait_recv()
    for e in (2, 3, 0, 1):
        piece = wacc[rows_of(RELAYS[e]), :]
        for i in range(3):
            piece = piece + drecv[i, e].astype(F32)
        hsend[e] = piece.astype(BF)
        wh(e).start()
    gk_out[...] = sum_ring(0)
    store_gk = pltpu.make_async_copy(gk_out, gk_hbm.at[0], lsem.at[8])
    store_gk.start()

    out = jnp.zeros((ROWS_OUT, HD), F32)
    for e in range(4):
        wh(e).wait_recv()
        out = out + hrecv[e].astype(F32)
    gw_hbm[...] = out

    for a in range(2):
        for i in range(6):
            ring(a, i).wait_send()
        for j in range(NZ):
            down_all(a, j, wait_send)
        for d in range(1, BLOCKS):
            up_if(a, d, wait_send)
        for j in range(1, NZ):
            over(a, j).wait_send()
    for o in range(1, NX):
        fetch(o).wait_send()
        spread(o).wait_send()
        for k in range(1, NT):
            share(o, k).wait_send()
    for i in range(3):
        wd(i).wait_send()
    for e in range(4):
        wh(e).wait_send()
    for store in (store_att, store_gq, store_gk):
        store.wait()


def hand_over(*refs):
    copies = [pltpu.make_async_copy(refs[i], refs[4 + i], refs[8].at[i]) for i in range(4)]
    for copy in copies:
        copy.start()
    for copy in copies:
        copy.wait()


def on_device(queries, keys, memory, value_weight, doc_ids, out_grad):
    vmem = pltpu.VMEM
    dma = pltpu.SemaphoreType.DMA
    anywhere = pl.BlockSpec(memory_space=pl.ANY)
    shape = jax.ShapeDtypeStruct
    outs = pl.pallas_call(
        kernel,
        out_shape=(
            shape((1, TOK, HEADS * HD), BF),
            shape((1, TOK, HEADS * HD), BF),
            shape((1, TOK, HD), BF),
            shape((ROWS_OUT, HD), F32),
        ),
        in_specs=[pl.BlockSpec(memory_space=pltpu.HBM)] * 6,
        out_specs=(pl.BlockSpec(memory_space=pltpu.VMEM),) * 4,
        scratch_shapes=[
            vmem((TOK, HEADS * HD), BF),
            vmem((TOK, HEADS * HD), BF),
            vmem((TOK, D), BF),
            vmem((D, HD), BF),
            vmem((1, SEQ), jnp.int32),
            vmem((2, SLOTS, TOK, HD), BF),
            vmem((LANES, HD), BF),
            vmem((LANES, HD), BF),
            vmem((LANES, HD), BF),
            vmem((HD, LANES), BF),
            vmem((HD, LANES), BF),
            vmem((D, TOK), BF),
            vmem((BLOCKS * TOK, LANES), F32),
            vmem((BLOCKS * TOK, LANES), BF),
            vmem((8, LANES), F32),
            vmem((8, LANES), F32),
            vmem((HD, LANES), F32),
            vmem((HD, LANES), F32),
            vmem((TOK, HEADS * HD), BF),
            vmem((TOK, HEADS * HD), BF),
            vmem((2, BLOCKS, TOK, HD), BF),
            vmem((2, BLOCKS, TOK, HD), BF),
            vmem((TOK, HD), F32),
            vmem((2, TOK, HD), F32),
            vmem((2, NZ, TOK, HD), BF),
            vmem((2, NZ, TOK, HD), BF),
            vmem((TOK, HD), BF),
            vmem((NX, TOK, HD), BF),
            vmem((NX, NT, ROWS_T, TOK), BF),
            vmem((NDP * ROWS_X, HD), F32),
            vmem((3, 4, ROWS_OUT, HD), BF),
            vmem((3, 4, ROWS_OUT, HD), BF),
            vmem((4, ROWS_OUT, HD), BF),
            vmem((4, ROWS_OUT, HD), BF),
            dma((10,)),
            dma((2, 6)), dma((2, 6)),
            dma((2, BLOCKS)), dma((2, BLOCKS)),
            dma((2, BLOCKS)), dma((2, BLOCKS)),
            dma((2, NZ)), dma((2, NZ)),
            dma((NX,)), dma((NX,)),
            dma((NX, NT)), dma((NX, NT)),
            dma((NX,)), dma((NX,)),
            dma((3,)), dma((3,)),
            dma((4,)), dma((4,)),
        ],
        compiler_params=pltpu.CompilerParams(
            collective_id=0, has_side_effects=True, vmem_limit_bytes=60 << 20
        ),
        name="cross_attention",
    )(queries, keys, memory, value_weight, doc_ids, out_grad)
    return pl.pallas_call(
        hand_over,
        out_shape=tuple(shape(o.shape, o.dtype) for o in outs),
        in_specs=[pl.BlockSpec(memory_space=pltpu.VMEM)] * 4,
        out_specs=(anywhere,) * 4,
        scratch_shapes=[dma((4,))],
        compiler_params=pltpu.CompilerParams(vmem_limit_bytes=60 << 20),
        name="hand_over",
    )(*outs)


def solution(mesh):
    in_specs = (
        P("dp", "context", "tensor"),
        P("dp", "context", "tensor"),
        P("dp", "context", None),
        P(None, "tensor"),
        P("dp", None),
        P("dp", "context", "tensor"),
    )
    out_specs = (
        P("dp", "context", "tensor"),
        P("dp", "context", "tensor"),
        P("dp", "context", "tensor"),
        P(("dp", "context"), "tensor"),
    )
    return jax.shard_map(
        on_device, mesh=mesh, in_specs=in_specs, out_specs=out_specs, check_vma=False
    )
```
